256 devices in a mesh: blk: 64 (over x, z, core), smp: 4 (over y).
Axes of the slice: x: 4, y: 4, z: 8, core: 2. Of those that a mesh axis runs over, the one named last changes fastest.
Arguments:
- encodings: bfloat16 [1024, 57344], P('smp', 'blk'), may hold values from -1 to 1
- hidden_pre: bfloat16 [1024, 8192], P('smp', 'blk'), may hold values from -6 to 6
- cotangent: bfloat16 [1024, 688128], P('smp', 'blk'), may hold values from -0.75 to 0.75
- out_weights: bfloat16 [10752, 128, 128], P('blk'), may hold values from -0.0390625 to 0.0390625
- out_contacts: int32 [5376, 2], P('blk'), may hold values from 0 to 63, all different within a row
- in_contacts: int32 [448, 4], P('blk'), may hold values from 0 to 63, all different within a row
Outputs:
- out_weight_grad: bfloat16 [10752, 128, 128], P(('blk', 'smp'))
- in_weight_grad: bfloat16 [1792, 128, 128], P(('blk', 'smp'))
The draws below stay inside these ranges and needn't reach their ends.
Inputs may be any that keep to these rules, and one draw needn't show every extreme that they name: `out_contacts`: each row names 2 different hidden blocks, and every hidden block is named by some row. `in_contacts`: each row names 4 different hidden blocks, and every hidden block is named by some row.
All inputs are finite; a program needn't handle non-finite values.
Results may differ from the reference program's by a relative error of at most 0.0051.
Values may be sent and summed in bfloat16 or wider, within the bound.
No kernel may reach another device: no remote copies, remote signals or barrier semaphores. Data moves between devices by JAX's collectives and lax.ppermute only.
A program may use at most 128 MiB of HBM per device.

```python
import jax
import jax.numpy as jnp
from jax import lax

BS = 128
H = 8192
K2 = 2
K1 = 4
OB_DEV = 84
IB_DEV = 7
NHB = 64
OUT_BLOCKS = 5376
IN_BLOCKS = 448
D_OUT = 688128
D_IN = 57344
NB2 = 10752
NB1 = 1792
SAMPLES = 1024
N_BLK = 64


def steps_of(own_key, shape, cuts, low, largest):
    loudness, own = 1.0, jax.random.fold_in(own_key, 6)
    for position, shards_of in cuts:
        heights = jnp.exp(jax.random.uniform(jax.random.fold_in(own, position), (shards_of,), jnp.float32, low / len(cuts), largest / len(cuts)))
        loudness = loudness * jnp.repeat(heights, shape[position] // shards_of).reshape([-1 if axis == position else 1 for axis in range(len(shape))])
    return loudness


def distinct(rng, rows, number_of, top, lift):
    ranking = jax.random.permutation(jax.random.fold_in(rng, 1), number_of)
    pull = ranking
    for power in range(3):
        pull = pull * pull // number_of
    pull = pull * lift // number_of
    chance = jax.random.randint(jax.random.fold_in(rng, 2), (rows, number_of), 0, 4096) + pull
    sure = jax.random.permutation(jax.random.fold_in(rng, 3), rows)[jnp.arange(number_of) % rows]
    chance = jnp.where(jnp.arange(rows)[:, None] == sure[None, :], 1 << 14, chance)
    priority = chance * number_of + jnp.arange(number_of)
    return lax.top_k(priority.astype(jnp.int32), top)[1].astype(jnp.int32)


def centred(key, shape, deviation, most, split=(), held_as=jnp.bfloat16):
    drawn = jax.random.normal(key, shape, jnp.float32) * deviation
    if len(split) > 0:
        drawn = steps_of(key, shape, split, -0.22, 0.18) * drawn
    return jnp.clip(drawn, min=-most, max=most).astype(held_as)


def setup_inputs(seed: int = 0) -> dict:
    arg_keys = jax.random.split(jax.random.key(seed), 7)
    return {
        "encodings": jnp.clip(jax.random.uniform(arg_keys[0], (SAMPLES, D_IN), jnp.float32, -1.0, 1.0) * steps_of(arg_keys[0], (SAMPLES, D_IN), ((0, 4), (1, 64)), -0.4, 0.0), -1.0, 1.0).astype(jnp.bfloat16),
        "hidden_pre": centred(arg_keys[1], (SAMPLES, H), 1.0, 6.0, ((0, 4), (1, 64))),
        "cotangent": centred(arg_keys[2], (SAMPLES, D_OUT), 0.05, 0.75, ((0, 4), (1, 64))),
        "out_weights": centred(arg_keys[3], (NB2, BS, BS), (OUT_BLOCKS * K2 * BS // NHB) ** -0.5, 0.0390625, ((0, 64),)),
        "out_contacts": distinct(arg_keys[4], OUT_BLOCKS, NHB, K2, 512),
        "in_contacts": distinct(arg_keys[5], IN_BLOCKS, NHB, K1, 512),
    }


def silu_slope(values):
    sigma = jax.nn.sigmoid(values)
    return sigma * (1.0 + values * (1.0 - sigma))


def reference(encodings, hidden_pre, cotangent, out_weights, out_contacts, in_contacts):
    sample_rows = cotangent.shape[0]
    pre_blocks = hidden_pre.astype(jnp.float32).reshape(sample_rows, NHB, BS)
    activation = lax.optimization_barrier(jax.nn.silu(pre_blocks).astype(jnp.bfloat16)).astype(jnp.float32)

    def out_step(carry, index):
        cot_slice = lax.dynamic_slice_in_dim(cotangent, index * (OB_DEV * BS), OB_DEV * BS, 1)
        cot_slice = cot_slice.astype(jnp.float32).reshape(sample_rows, OB_DEV, BS)
        weight_slice = lax.dynamic_slice_in_dim(out_weights, index * (OB_DEV * K2), OB_DEV * K2, 0)
        weight_slice = weight_slice.astype(jnp.float32).reshape(OB_DEV, K2, BS, BS)
        contact_slice = lax.dynamic_slice_in_dim(out_contacts, index * OB_DEV, OB_DEV, 0).reshape(-1).astype(jnp.int32)
        taken = jnp.take(activation, contact_slice, axis=1).reshape(sample_rows, OB_DEV, K2, BS)
        grad_slice = jnp.einsum("sokb,soc->okbc", taken, cot_slice, precision=lax.Precision.HIGHEST)
        grad_slice = grad_slice.reshape(OB_DEV * K2, BS, BS).astype(jnp.bfloat16)
        partial_terms = jnp.einsum("soc,okbc->oksb", cot_slice, weight_slice, precision=lax.Precision.HIGHEST)
        partial_terms = partial_terms.reshape(OB_DEV * K2, sample_rows, BS)
        carry = carry + jax.ops.segment_sum(partial_terms, contact_slice, num_segments=NHB)
        return carry, grad_slice

    start = jnp.zeros((NHB, sample_rows, BS), jnp.float32)
    summed, out_grad = lax.scan(out_step, start, jnp.arange(N_BLK, dtype=jnp.int32))
    grad_pre = (jnp.swapaxes(summed, 0, 1) * silu_slope(pre_blocks)).astype(jnp.bfloat16)
    grad_wide = lax.optimization_barrier(grad_pre).astype(jnp.float32)

    def in_step(index):
        enc_slice = lax.dynamic_slice_in_dim(encodings, index * (IB_DEV * BS), IB_DEV * BS, 1)
        enc_slice = enc_slice.astype(jnp.float32).reshape(sample_rows, IB_DEV, BS)
        contact_slice = lax.dynamic_slice_in_dim(in_contacts, index * IB_DEV, IB_DEV, 0).reshape(-1).astype(jnp.int32)
        taken = jnp.take(grad_wide, contact_slice, axis=1).reshape(sample_rows, IB_DEV, K1, BS)
        result = jnp.einsum("sib,sikc->ikbc", enc_slice, taken, precision=lax.Precision.HIGHEST)
        return result.reshape(IB_DEV * K1, BS, BS).astype(jnp.bfloat16)

    in_grad = lax.map(in_step, jnp.arange(N_BLK, dtype=jnp.int32))
    return out_grad.reshape(NB2, BS, BS), in_grad.reshape(NB1, BS, BS)
```

```python
import jax
import jax.numpy as jnp
from jax import lax
from jax.experimental import pallas as pl
from jax.experimental.pallas import tpu as pltpu
from jax.sharding import PartitionSpec as P

BF16 = jnp.bfloat16
F32 = jnp.float32
NX, NZ, NC, NY = 4, 8, 2, 4
BS = 128
STEP_BLOCKS = 7
VMEM = 56 * 2**20


def index_of(x, z, core):
    return ((x % NX) * NZ + z % NZ) * NC + core % NC


def moved(value, dx=0, dz=0, dc=0):
    pairs = [
        (index_of(x, z, c), index_of(x + dx, z + dz, c + dc))
        for x in range(NX)
        for z in range(NZ)
        for c in range(NC)
    ]
    return lax.ppermute(value, "blk", pairs)


def moved_smp(value, dy):
    return lax.ppermute(value, "smp", [(i, (i + dy) % NY) for i in range(NY)])


def params(**more):
    return pltpu.CompilerParams(vmem_limit_bytes=VMEM, **more)


def contract(lhs, rhs, over):
    return lax.dot_general(lhs, rhs, ((over[:1], over[1:]), ((), ())), preferred_element_type=F32)


def after(value, other):
    anywhere = pl.BlockSpec(memory_space=pl.ANY)
    return pl.pallas_call(
        lambda *refs: None,
        in_specs=[anywhere, anywhere],
        out_specs=anywhere,
        out_shape=jax.ShapeDtypeStruct(value.shape, value.dtype),
        input_output_aliases={0: 0},
        name="after",
    )(value, other)


def hidden_kernel(place, contacts, cot_ref, weight_ref, send_ref, keep_ref, total):
    step = pl.program_id(0)
    core = place[2]

    @pl.when(step == 0)
    def _():
        total[...] = jnp.zeros_like(total)

    for o in range(STEP_BLOCKS):
        cot = cot_ref[:, o * BS : (o + 1) * BS]
        weights = weight_ref[2 * o : 2 * o + 2].reshape(2 * BS, BS)
        terms = contract(cot, weights, (1, 1))
        for m in range(2):
            k = contacts[m, step * STEP_BLOCKS + o]
            total[k] += terms[:, m * BS : (m + 1) * BS]

    @pl.when(step == pl.num_programs(0) - 1)
    def _():
        def write(p, carry):
            send_ref[p] = total[2 * p + 1 - core].astype(BF16)
            keep_ref[p] = total[2 * p + core]
            return carry

        lax.fori_loop(0, NX * NZ, write, 0)


def hidden_sums(place, contacts, cotangent, weights):
    rows = cotangent.shape[0]
    count = NX * NZ
    steps = weights.shape[0] // (2 * STEP_BLOCKS)
    return pl.pallas_call(
        hidden_kernel,
        grid_spec=pltpu.PrefetchScalarGridSpec(
            num_scalar_prefetch=2,
            grid=(steps,),
            in_specs=[
                pl.BlockSpec((rows, STEP_BLOCKS * BS), lambda g, *_: (0, g)),
                pl.BlockSpec((2 * STEP_BLOCKS, BS, BS), lambda g, *_: (g, 0, 0)),
            ],
            out_specs=[
                pl.BlockSpec((count, rows, BS), lambda g, *_: (0, 0, 0)),
                pl.BlockSpec((count, rows, BS), lambda g, *_: (0, 0, 0)),
            ],
            scratch_shapes=[pltpu.VMEM((2 * count, rows, BS), F32)],
        ),
        out_shape=[
            jax.ShapeDtypeStruct((count, rows, BS), BF16),
            jax.ShapeDtypeStruct((count, rows, BS), F32),
        ],
        compiler_params=params(),
        cost_estimate=pl.CostEstimate(flops=3 * 10**9, bytes_accessed=2**24, transcendentals=0),
        name="hidden_sums",
    )(place, contacts, cotangent, weights)


def core_kernel(place, keep_ref, got_ref, *outs):
    x = place[0]
    for d in range(NX):
        at = (x + d) & (NX - 1)
        outs[d][0] = (keep_ref[at, 0] + got_ref[at, 0].astype(F32)).astype(outs[d].dtype)


def core_sums(place, keep, got):
    rows = keep.shape[1]
    spec = pl.BlockSpec((NX, 1, rows, BS), lambda g, *_: (0, g, 0, 0))
    return pl.pallas_call(
        core_kernel,
        grid_spec=pltpu.PrefetchScalarGridSpec(
            num_scalar_prefetch=1,
            grid=(NZ,),
            in_specs=[spec, spec],
            out_specs=[pl.BlockSpec((1, rows, BS), lambda g, *_: (g, 0, 0))] * NX,
        ),
        out_shape=[
            jax.ShapeDtypeStruct((NZ, rows, BS), BF16 if d else F32) for d in range(NX)
        ],
        compiler_params=params(),
        cost_estimate=pl.CostEstimate(flops=10**6, bytes_accessed=2**23, transcendentals=0),
        name="core_sums",
    )(place, keep.reshape(NX, NZ, rows, BS), got.reshape(NX, NZ, rows, BS))


def line_kernel(place, keep_ref, a_ref, b_ref, c_ref, *outs):
    z = place[1]
    for d in range(NZ):
        at = (z + d) & (NZ - 1)
        total = keep_ref[at] + a_ref[at].astype(F32) + b_ref[at].astype(F32) + c_ref[at].astype(F32)
        outs[d][...] = total.astype(outs[d].dtype)


def line_sums(place, keep, *got):
    rows = keep.shape[1]
    whole = pl.BlockSpec(memory_space=pltpu.VMEM)
    return pl.pallas_call(
        line_kernel,
        in_specs=[pl.BlockSpec(memory_space=pltpu.SMEM)] + [whole] * NX,
        out_specs=[whole] * NZ,
        out_shape=[jax.ShapeDtypeStruct((rows, BS), BF16 if d else F32) for d in range(NZ)],
        compiler_params=params(),
        cost_estimate=pl.CostEstimate(flops=10**6, bytes_accessed=2**22, transcendentals=0),
        name="line_sums",
    )(place, keep, *got)


def out_kernel(place, contacts, cot_ref, own_ref, other_ref, out_ref, held, sems):
    step = pl.program_id(0)
    x, core = place[0], place[2]

    @pl.when(step == 0)
    def _():
        copies = [
            pltpu.make_async_copy(own_ref, held.at[core], sems.at[0]),
            pltpu.make_async_copy(other_ref, held.at[1 - core], sems.at[1]),
        ]
        for copy in copies:
            copy.start()
        for copy in copies:
            copy.wait()

    for o in range(STEP_BLOCKS):
        cot = cot_ref[:, o * BS : (o + 1) * BS]
        for m in range(2):
            k = contacts[m, step * STEP_BLOCKS + o]
            slot = ((k >> 1) & (NZ - 1)) * NX + ((x - (k >> 4)) & (NX - 1))
            out_ref[2 * o + m] = contract(held[k & 1, slot], cot, (1, 0)).astype(BF16)


def out_terms(place, contacts, cotangent, own, other):
    rows = cotangent.shape[0]
    count = contacts.shape[1]
    return pl.pallas_call(
        out_kernel,
        grid_spec=pltpu.PrefetchScalarGridSpec(
            num_scalar_prefetch=2,
            grid=(count // STEP_BLOCKS,),
            in_specs=[
                pl.BlockSpec((rows, STEP_BLOCKS * BS), lambda g, *_: (0, g)),
                pl.BlockSpec(memory_space=pl.ANY),
                pl.BlockSpec(memory_space=pl.ANY),
            ],
            out_specs=pl.BlockSpec((2 * STEP_BLOCKS, BS, BS), lambda g, *_: (g, 0, 0)),
            scratch_shapes=[
                pltpu.VMEM((NC, NX * NZ, BS, rows), BF16),
                pltpu.SemaphoreType.DMA((2,)),
            ],
        ),
        out_shape=jax.ShapeDtypeStruct((2 * count, BS, BS), BF16),
        compiler_params=params(),
        cost_estimate=pl.CostEstimate(flops=3 * 10**9, bytes_accessed=2**24, transcendentals=0),
        name="out_terms",
    )(place, contacts, cotangent, own, other)


def in_kernel(place, contacts, enc_ref, *refs):
    parts, outs, (held, made, sems) = refs[: NC * NX], refs[NC * NX : NC * NX + NY], refs[NC * NX + NY :]
    x, z, core, y = place[0], place[1], place[2], place[3]
    copies = [
        pltpu.make_async_copy(part, held.at[n], sems.at[n]) for n, part in enumerate(parts)
    ]
    for copy in copies:
        copy.start()
    for copy in copies:
        copy.wait()
    per_in, count = contacts.shape
    for i in range(count):
        turned = enc_ref[:, i * BS : (i + 1) * BS].T
        for m in range(per_in):
            k = contacts[m, i]
            slot = ((k & 1) ^ core) * NX + ((x - (k >> 4)) & (NX - 1))
            value = held[slot, (z - (k >> 1)) & (NZ - 1)]
            made[i * per_in + m] = contract(turned, value, (1, 0))
    each = count * per_in // NY
    for d in range(NY):
        first = ((y + d) & (NY - 1)) * each
        for n in range(each):
            outs[d][n] = made[first + n].astype(outs[d].dtype)


def in_terms(place, contacts, encodings, parts):
    rows = encodings.shape[0]
    per_in, count = contacts.shape
    each = per_in * count // NY
    smem = pl.BlockSpec(memory_space=pltpu.SMEM)
    whole = pl.BlockSpec(memory_space=pltpu.VMEM)
    return pl.pallas_call(
        in_kernel,
        in_specs=[smem, smem, whole] + [pl.BlockSpec(memory_space=pl.ANY)] * (NC * NX),
        out_specs=[whole] * NY,
        scratch_shapes=[
            pltpu.VMEM((NC * NX, NZ, rows, BS), BF16),
            pltpu.VMEM((per_in * count, BS, BS), F32),
            pltpu.SemaphoreType.DMA((NC * NX,)),
        ],
        out_shape=[jax.ShapeDtypeStruct((each, BS, BS), BF16 if d else F32) for d in range(NY)],
        compiler_params=params(),
        cost_estimate=pl.CostEstimate(flops=5 * 10**8, bytes_accessed=2**23, transcendentals=0),
        name="in_terms",
    )(place, contacts, encodings, *parts)


def silu_slope(values):
    sigma = jax.nn.sigmoid(values)
    return sigma * (1.0 + values * (1.0 - sigma))


def per_device(encodings, hidden_pre, cotangent, out_weights, out_contacts, in_contacts):
    position = lax.axis_index("blk")
    place = jnp.stack(
        [position // (NZ * NC), position // NC % NZ, position % NC, lax.axis_index("smp")]
    ).astype(jnp.int32)
    out_index, in_index = out_contacts.T, in_contacts.T
    pre = hidden_pre.astype(F32)

    activation = jax.nn.silu(pre).astype(BF16).T
    along_x = jnp.stack([activation] + [moved(activation, dx=d) for d in range(1, NX)])
    lines = [[index_of(x, z, c) for z in range(NZ)] for x in range(NX) for c in range(NC)]
    act_own = lax.all_gather(along_x, "blk", axis_index_groups=lines)
    act_own = act_own.reshape(NZ * NX, BS, -1)

    send, keep = hidden_sums(place, out_index, cotangent, out_weights)

    by_x = core_sums(place, keep, moved(send, dc=1))
    by_z = line_sums(place, by_x[0], *[moved(by_x[d], dx=d) for d in range(1, NX)])
    act_own = after(act_own, by_z[0])
    got = [moved(by_z[d], dz=d) for d in range(1, NZ)]
    grad_act = sum((g.astype(F32) for g in got), by_z[0])
    grad_pre = (grad_act * silu_slope(pre)).astype(BF16)

    along_z = jnp.stack([grad_pre] + [moved(grad_pre, dz=d) for d in range(1, NZ)])
    own = [along_z] + [moved(along_z, dx=d) for d in range(1, NX)]
    parts = own + [moved(part, dc=1) for part in own]

    terms = out_terms(place, out_index, cotangent, act_own, moved(act_own, dc=1))
    out_grad = lax.psum_scatter(terms, "smp", scatter_dimension=0, tiled=True)

    mine, *away = in_terms(place, in_index, encodings, parts)
    in_grad = sum((moved_smp(a, d + 1).astype(F32) for d, a in enumerate(away)), mine)
    return (out_grad, in_grad.astype(BF16))


def solution(mesh):
    in_specs = (
        P("smp", "blk"),
        P("smp", "blk"),
        P("smp", "blk"),
        P("blk", None, None),
        P("blk", None),
        P("blk", None),
    )
    out_specs = (P(("blk", "smp"), None, None), P(("blk", "smp"), None, None))
    return jax.shard_map(
        per_device, mesh=mesh, in_specs=in_specs, out_specs=out_specs, check_vma=False
    )
```

```python
import jax
import jax.numpy as jnp
from jax import lax
from jax.experimental import pallas as pl
from jax.experimental.pallas import tpu as pltpu
from jax.sharding import PartitionSpec as P

BF16 = jnp.bfloat16
F32 = jnp.float32
NX, NZ, NC, NY = 4, 8, 2, 4
BS = 128
STEP_BLOCKS = 28
OUT_STEP = 28
CORE_STEP = 2


def index_of(x, z, core):
    return ((x % NX) * NZ + z % NZ) * NC + core % NC


def moved(value, dx=0, dz=0, dc=0):
    pairs = [
        (index_of(x, z, c), index_of(x + dx, z + dz, c + dc))
        for x in range(NX)
        for z in range(NZ)
        for c in range(NC)
    ]
    return lax.ppermute(value, "blk", pairs)


LINES = [[index_of(x, z, c) for z in range(NZ)] for x in range(NX) for c in range(NC)]


def params(mib):
    return pltpu.CompilerParams(vmem_limit_bytes=mib * 2**20)


def contract(lhs, rhs, over):
    return lax.dot_general(lhs, rhs, ((over[:1], over[1:]), ((), ())), preferred_element_type=F32)


def after(value, other):
    anywhere = pl.BlockSpec(memory_space=pl.ANY)
    return pl.pallas_call(
        lambda *refs: None,
        in_specs=[anywhere, anywhere],
        out_specs=anywhere,
        out_shape=jax.ShapeDtypeStruct(value.shape, value.dtype),
        input_output_aliases={0: 0},
        name="after",
    )(value, other)


def hidden_kernel(place, contacts, cot_ref, weight_ref, send_ref, keep_ref, total):
    step = pl.program_id(0)
    core = place[2]

    @pl.when(step == 0)
    def _():
        total[...] = jnp.zeros_like(total)

    for o in range(STEP_BLOCKS):
        cot = cot_ref[:, o * BS : (o + 1) * BS]
        weights = weight_ref[2 * o : 2 * o + 2].reshape(2 * BS, BS)
        terms = contract(cot, weights, (1, 1))
        for m in range(2):
            k = contacts[m, step * STEP_BLOCKS + o]
            total[k] += terms[:, m * BS : (m + 1) * BS]

    @pl.when(step == pl.num_programs(0) - 1)
    def _():
        def write(p, carry):
            send_ref[p] = total[2 * p + 1 - core].astype(BF16)
            keep_ref[p] = total[2 * p + core]
            return carry

        lax.fori_loop(0, NX * NZ, write, 0)


def hidden_sums(place, contacts, cotangent, weights):
    rows = cotangent.shape[0]
    count = NX * NZ
    steps = weights.shape[0] // (2 * STEP_BLOCKS)
    return pl.pallas_call(
        hidden_kernel,
        grid_spec=pltpu.PrefetchScalarGridSpec(
            num_scalar_prefetch=2,
            grid=(steps,),
            in_specs=[
                pl.BlockSpec((rows, STEP_BLOCKS * BS), lambda g, *_: (0, g)),
                pl.BlockSpec((2 * STEP_BLOCKS, BS, BS), lambda g, *_: (g, 0, 0)),
            ],
            out_specs=[
                pl.BlockSpec((count, rows, BS), lambda g, *_: (0, 0, 0)),
                pl.BlockSpec((count, rows, BS), lambda g, *_: (0, 0, 0)),
            ],
            scratch_shapes=[pltpu.VMEM((2 * count, rows, BS), F32)],
        ),
        out_shape=[
            jax.ShapeDtypeStruct((count, rows, BS), BF16),
            jax.ShapeDtypeStruct((count, rows, BS), F32),
        ],
        compiler_params=params(56),
        cost_estimate=pl.CostEstimate(flops=3 * 10**9, bytes_accessed=2**24, transcendentals=0),
        name="hidden_sums",
    )(place, contacts, cotangent, weights)


def core_kernel(place, keep_ref, got_ref, *outs):
    x = place[0]
    for d in range(NX):
        at = (x + d) & (NX - 1)
        for n in range(CORE_STEP):
            outs[d][n] = (keep_ref[at, n] + got_ref[at, n].astype(F32)).astype(outs[d].dtype)


def core_sums(place, keep, got):
    rows = keep.shape[1]
    spec = pl.BlockSpec((NX, CORE_STEP, rows, BS), lambda g, *_: (0, g, 0, 0))
    return pl.pallas_call(
        core_kernel,
        grid_spec=pltpu.PrefetchScalarGridSpec(
            num_scalar_prefetch=1,
            grid=(NZ // CORE_STEP,),
            in_specs=[spec, spec],
            out_specs=[pl.BlockSpec((CORE_STEP, rows, BS), lambda g, *_: (g, 0, 0))] * NX,
        ),
        out_shape=[
            jax.ShapeDtypeStruct((NZ, rows, BS), BF16 if d else F32) for d in range(NX)
        ],
        compiler_params=params(16),
        cost_estimate=pl.CostEstimate(flops=10**6, bytes_accessed=2**23, transcendentals=0),
        name="core_sums",
    )(place, keep.reshape(NX, NZ, rows, BS), got.reshape(NX, NZ, rows, BS))


def line_kernel(place, keep_ref, a_ref, b_ref, c_ref, send_ref, own_ref):
    def total(at):
        return keep_ref[at] + a_ref[at].astype(F32) + b_ref[at].astype(F32) + c_ref[at].astype(F32)

    for at in range(NZ):
        send_ref[at] = total(at).astype(BF16)
    own_ref[...] = total(place[1])


def line_sums(place, keep, *got):
    rows = keep.shape[1]
    whole = pl.BlockSpec(memory_space=pltpu.VMEM)
    return pl.pallas_call(
        line_kernel,
        in_specs=[pl.BlockSpec(memory_space=pltpu.SMEM)] + [whole] * NX,
        out_specs=[whole] * 2,
        out_shape=[
            jax.ShapeDtypeStruct((NZ, rows, BS), BF16),
            jax.ShapeDtypeStruct((rows, BS), F32),
        ],
        compiler_params=params(8),
        cost_estimate=pl.CostEstimate(flops=10**6, bytes_accessed=2**22, transcendentals=0),
        name="line_sums",
    )(place, keep, *got)


def out_kernel(place, contacts, cot_ref, own_ref, other_ref, out_ref, held, sems):
    step = pl.program_id(0)
    x, core = place[0], place[2]

    @pl.when(step == 0)
    def _():
        copies = [
            pltpu.make_async_copy(own_ref, held.at[core], sems.at[0]),
            pltpu.make_async_copy(other_ref, held.at[1 - core], sems.at[1]),
        ]
        for copy in copies:
            copy.start()
        for copy in copies:
            copy.wait()

    def block(k):
        return held[k & 1, ((k >> 1) & (NZ - 1)) * NX + ((x - (k >> 4)) & (NX - 1))]

    for o in range(OUT_STEP):
        pair = [block(contacts[m, step * OUT_STEP + o]) for m in range(2)]
        cot = cot_ref[:, o * BS : (o + 1) * BS]
        terms = contract(jnp.concatenate(pair), cot, (1, 0)).astype(BF16)
        out_ref[2 * o : 2 * o + 2] = terms.reshape(2, BS, BS)


def out_terms(place, contacts, cotangent, own, other):
    rows = cotangent.shape[0]
    count = contacts.shape[1]
    return pl.pallas_call(
        out_kernel,
        grid_spec=pltpu.PrefetchScalarGridSpec(
            num_scalar_prefetch=2,
            grid=(count // OUT_STEP,),
            in_specs=[
                pl.BlockSpec((rows, OUT_STEP * BS), lambda g, *_: (0, g)),
                pl.BlockSpec(memory_space=pl.ANY),
                pl.BlockSpec(memory_space=pl.ANY),
            ],
            out_specs=pl.BlockSpec((2 * OUT_STEP, BS, BS), lambda g, *_: (g, 0, 0)),
            scratch_shapes=[
                pltpu.VMEM((NC, NX * NZ, BS, rows), BF16),
                pltpu.SemaphoreType.DMA((2,)),
            ],
        ),
        out_shape=jax.ShapeDtypeStruct((2 * count, BS, BS), BF16),
        compiler_params=params(56),
        cost_estimate=pl.CostEstimate(flops=3 * 10**9, bytes_accessed=2**24, transcendentals=0),
        name="out_terms",
    )(place, contacts, cotangent, own, other)


def in_kernel(place, contacts, enc_ref, *refs):
    parts, (send_ref, mine_ref, held, made, sems) = refs[: NC * NX], refs[NC * NX :]
    x, core, y = place[0], place[2], place[3]
    copies = [
        pltpu.make_async_copy(part, held.at[n], sems.at[n]) for n, part in enumerate(parts)
    ]
    for copy in copies:
        copy.start()
    for copy in copies:
        copy.wait()
    per_in, count = contacts.shape
    for i in range(count):
        turned = enc_ref[:, i * BS : (i + 1) * BS].T
        for m in range(per_in):
            k = contacts[m, i]
            slot = ((k & 1) ^ core) * NX + ((x - (k >> 4)) & (NX - 1))
            made[i * per_in + m] = contract(turned, held[slot, (k >> 1) & (NZ - 1)], (1, 0))
    for n in range(count * per_in):
        send_ref[n] = made[n].astype(BF16)
    each = count * per_in // NY
    for n in range(each):
        mine_ref[n] = made[y * each + n]


def in_terms(place, contacts, encodings, parts):
    rows = encodings.shape[0]
    per_in, count = contacts.shape
    each = per_in * count // NY
    smem = pl.BlockSpec(memory_space=pltpu.SMEM)
    whole = pl.BlockSpec(memory_space=pltpu.VMEM)
    return pl.pallas_call(
        in_kernel,
        in_specs=[smem, smem, whole] + [pl.BlockSpec(memory_space=pl.ANY)] * (NC * NX),
        out_specs=[whole] * 2,
        scratch_shapes=[
            pltpu.VMEM((NC * NX, NZ, rows, BS), BF16),
            pltpu.VMEM((per_in * count, BS, BS), F32),
            pltpu.SemaphoreType.DMA((NC * NX,)),
        ],
        out_shape=[
            jax.ShapeDtypeStruct((per_in * count, BS, BS), BF16),
            jax.ShapeDtypeStruct((each, BS, BS), F32),
        ],
        compiler_params=params(14),
        cost_estimate=pl.CostEstimate(flops=5 * 10**8, bytes_accessed=2**23, transcendentals=0),
        name="in_terms",
    )(place, contacts, encodings, *parts)


def sum_parts(parts, own, at):
    which = lax.broadcasted_iota(jnp.int32, parts.shape, 0)
    return jnp.sum(jnp.where(which == at, own[None], parts.astype(F32)), axis=0)


def silu_slope(values):
    sigma = jax.nn.sigmoid(values)
    return sigma * (1.0 + values * (1.0 - sigma))


def per_device(encodings, hidden_pre, cotangent, out_weights, out_contacts, in_contacts):
    position = lax.axis_index("blk")
    place = jnp.stack(
        [position // (NZ * NC), position // NC % NZ, position % NC, lax.axis_index("smp")]
    ).astype(jnp.int32)
    out_index, in_index = out_contacts.T, in_contacts.T
    pre = hidden_pre.astype(F32)

    activation = jax.nn.silu(pre).astype(BF16).T
    arrived = [moved(activation, dx=d) for d in range(1, NX)]

    send, keep = hidden_sums(place, out_index, cotangent, out_weights)
    along_x = jnp.stack([after(activation, send)] + arrived)
    send = after(send, along_x)
    act_own = lax.all_gather(along_x, "blk", axis_index_groups=LINES)
    act_own = act_own.reshape(NZ * NX, BS, -1)

    by_x = core_sums(place, keep, moved(send, dc=1))
    by_z, own_z = line_sums(place, by_x[0], *[moved(by_x[d], dx=d) for d in range(1, NX)])
    got = lax.all_to_all(by_z, "blk", 0, 0, axis_index_groups=LINES)
    grad_pre = (sum_parts(got, own_z, place[1]) * silu_slope(pre)).astype(BF16)

    act_own = after(act_own, by_z)
    terms = out_terms(place, out_index, cotangent, act_own, moved(act_own, dc=1))
    out_grad = lax.psum_scatter(terms, "smp", scatter_dimension=0, tiled=True)

    copies = jnp.broadcast_to(grad_pre, (NZ, *grad_pre.shape))
    along_z = lax.all_to_all(copies, "blk", 0, 0, axis_index_groups=LINES)
    own = [along_z] + [moved(along_z, dx=d) for d in range(1, NX)]
    parts = own + [moved(part, dc=1) for part in own]

    away, mine = in_terms(place, in_index, encodings, parts)
    away = away.reshape(NY, *mine.shape)
    away = lax.all_to_all(away, "smp", 0, 0)
    in_grad = sum_parts(away, mine, place[3]).astype(BF16)
    return (out_grad, in_grad)


def solution(mesh):
    in_specs = (
        P("smp", "blk"),
        P("smp", "blk"),
        P("smp", "blk"),
        P("blk", None, None),
        P("blk", None),
        P("blk", None),
    )
    out_specs = (P(("blk", "smp"), None, None), P(("blk", "smp"), None, None))
    return jax.shard_map(
        per_device, mesh=mesh, in_specs=in_specs, out_specs=out_specs, check_vma=False
    )
```

```python
import jax
import jax.numpy as jnp
from jax import lax
from jax.experimental import pallas as pl
from jax.experimental.pallas import tpu as pltpu
from jax.sharding import PartitionSpec as P

BF16 = jnp.bfloat16
F32 = jnp.float32
NX, NZ, NC, NY = 4, 8, 2, 4
BS = 128
STEP_BLOCKS = 28
OUT_STEP = 28
CORE_STEP = 2
FIRST, LAST = 176, 80


def index_of(x, z, core):
    return ((x % NX) * NZ + z % NZ) * NC + core % NC


def moved(value, dx=0, dz=0, dc=0):
    pairs = [
        (index_of(x, z, c), index_of(x + dx, z + dz, c + dc))
        for x in range(NX)
        for z in range(NZ)
        for c in range(NC)
    ]
    return lax.ppermute(value, "blk", pairs)


LINES = [[index_of(x, z, c) for z in range(NZ)] for x in range(NX) for c in range(NC)]


def params(mib):
    return pltpu.CompilerParams(vmem_limit_bytes=mib * 2**20)


def contract(lhs, rhs, over):
    return lax.dot_general(lhs, rhs, ((over[:1], over[1:]), ((), ())), preferred_element_type=F32)


def after(value, other):
    anywhere = pl.BlockSpec(memory_space=pl.ANY)
    other = other[(0,) * (other.ndim - 2)][:16]
    return pl.pallas_call(
        lambda *refs: None,
        in_specs=[anywhere, anywhere],
        out_specs=anywhere,
        out_shape=jax.ShapeDtypeStruct(value.shape, value.dtype),
        input_output_aliases={0: 0},
        compiler_params=params(56),
        name="after",
    )(value, other)


def hidden_kernel(place, contacts, cot_ref, weight_ref, send_ref, keep_ref, total):
    step = pl.program_id(0)
    core = place[2]

    @pl.when(step == 0)
    def _():
        total[...] = jnp.zeros_like(total)

    for o in range(STEP_BLOCKS):
        cot = cot_ref[:, o * BS : (o + 1) * BS]
        weights = weight_ref[2 * o : 2 * o + 2].reshape(2 * BS, BS)
        terms = contract(cot, weights, (1, 1))
        for m in range(2):
            k = contacts[m, step * STEP_BLOCKS + o]
            total[k] += terms[:, m * BS : (m + 1) * BS]

    @pl.when(step == pl.num_programs(0) - 1)
    def _():
        def write(p, carry):
            send_ref[p] = total[2 * p + 1 - core].astype(BF16)
            keep_ref[p] = total[2 * p + core]
            return carry

        lax.fori_loop(0, NX * NZ, write, 0)


def hidden_sums(place, contacts, cotangent, weights):
    rows = cotangent.shape[0]
    count = NX * NZ
    steps = weights.shape[0] // (2 * STEP_BLOCKS)
    return pl.pallas_call(
        hidden_kernel,
        grid_spec=pltpu.PrefetchScalarGridSpec(
            num_scalar_prefetch=2,
            grid=(steps,),
            in_specs=[
                pl.BlockSpec((rows, STEP_BLOCKS * BS), lambda g, *_: (0, g)),
                pl.BlockSpec((2 * STEP_BLOCKS, BS, BS), lambda g, *_: (g, 0, 0)),
            ],
            out_specs=[
                pl.BlockSpec((count, rows, BS), lambda g, *_: (0, 0, 0)),
                pl.BlockSpec((count, rows, BS), lambda g, *_: (0, 0, 0)),
            ],
            scratch_shapes=[pltpu.VMEM((2 * count, rows, BS), F32)],
        ),
        out_shape=[
            jax.ShapeDtypeStruct((count, rows, BS), BF16),
            jax.ShapeDtypeStruct((count, rows, BS), F32),
        ],
        compiler_params=params(56),
        cost_estimate=pl.CostEstimate(flops=3 * 10**9, bytes_accessed=2**24, transcendentals=0),
        name="hidden_sums",
    )(place, contacts, cotangent, weights)


def core_kernel(place, keep_ref, got_ref, *outs):
    x, z = place[0], place[1]
    step = pl.program_id(0)
    z_send, z_own = outs[NX:]

    def last(at, n):
        return keep_ref[at, n, FIRST:] + got_ref[at, n, FIRST:].astype(F32)

    for n in range(CORE_STEP):
        for d in range(NX):
            at = (x + d) & (NX - 1)
            total = keep_ref[at, n, :FIRST] + got_ref[at, n, :FIRST].astype(F32)
            outs[d][n] = total.astype(outs[d].dtype)
            z_send[n, d] = last(d, n).astype(BF16)

        @pl.when(step * CORE_STEP + n == z)
        def _():
            for d in range(NX):
                z_own[d] = last(d, n)


def core_sums(place, keep, got):
    rows = keep.shape[1]
    spec = pl.BlockSpec((NX, CORE_STEP, rows, BS), lambda g, *_: (0, g, 0, 0))
    return pl.pallas_call(
        core_kernel,
        grid_spec=pltpu.PrefetchScalarGridSpec(
            num_scalar_prefetch=1,
            grid=(NZ // CORE_STEP,),
            in_specs=[spec, spec],
            out_specs=[pl.BlockSpec((CORE_STEP, FIRST, BS), lambda g, *_: (g, 0, 0))] * NX
            + [
                pl.BlockSpec((CORE_STEP, NX, LAST, BS), lambda g, *_: (g, 0, 0, 0)),
                pl.BlockSpec((NX, LAST, BS), lambda g, *_: (0, 0, 0)),
            ],
        ),
        out_shape=[
            jax.ShapeDtypeStruct((NZ, FIRST, BS), BF16 if d else F32) for d in range(NX)
        ]
        + [
            jax.ShapeDtypeStruct((NZ, NX, LAST, BS), BF16),
            jax.ShapeDtypeStruct((NX, LAST, BS), F32),
        ],
        compiler_params=params(16),
        cost_estimate=pl.CostEstimate(flops=10**6, bytes_accessed=2**23, transcendentals=0),
        name="core_sums",
    )(place, keep.reshape(NX, NZ, rows, BS), got.reshape(NX, NZ, rows, BS))


def line_kernel(place, keep_ref, a_ref, b_ref, c_ref, send_ref, own_ref):
    def total(at):
        return keep_ref[at] + a_ref[at].astype(F32) + b_ref[at].astype(F32) + c_ref[at].astype(F32)

    for at in range(NZ):
        send_ref[at] = total(at).astype(BF16)
    own_ref[...] = total(place[1])


def line_sums(place, keep, *got):
    whole = pl.BlockSpec(memory_space=pltpu.VMEM)
    return pl.pallas_call(
        line_kernel,
        in_specs=[pl.BlockSpec(memory_space=pltpu.SMEM)] + [whole] * NX,
        out_specs=[whole] * 2,
        out_shape=[
            jax.ShapeDtypeStruct((NZ, FIRST, BS), BF16),
            jax.ShapeDtypeStruct((FIRST, BS), F32),
        ],
        compiler_params=params(8),
        cost_estimate=pl.CostEstimate(flops=10**6, bytes_accessed=2**22, transcendentals=0),
        name="line_sums",
    )(place, keep, *got)


def plane_kernel(place, own_ref, got_ref, *outs):
    x, z = place[0], place[1]
    for d in range(NX):
        at = (x + d) & (NX - 1)
        total = own_ref[at]
        for n in range(NZ):
            total += jnp.where(z == n, 0.0, got_ref[n, at].astype(F32))
        outs[d][...] = total.astype(outs[d].dtype)


def plane_sums(place, own, got):
    whole = pl.BlockSpec(memory_space=pltpu.VMEM)
    return pl.pallas_call(
        plane_kernel,
        in_specs=[pl.BlockSpec(memory_space=pltpu.SMEM), whole, whole],
        out_specs=[whole] * NX,
        out_shape=[jax.ShapeDtypeStruct((LAST, BS), BF16 if d else F32) for d in range(NX)],
        compiler_params=params(8),
        cost_estimate=pl.CostEstimate(flops=10**6, bytes_accessed=2**20, transcendentals=0),
        name="plane_sums",
    )(place, own, got)


def out_kernel(place, contacts, cot_ref, own_ref, other_ref, out_ref, held, sems):
    step = pl.program_id(0)
    x, core = place[0], place[2]

    @pl.when(step == 0)
    def _():
        copies = [
            pltpu.make_async_copy(own_ref, held.at[core], sems.at[0]),
            pltpu.make_async_copy(other_ref, held.at[1 - core], sems.at[1]),
        ]
        for copy in copies:
            copy.start()
        for copy in copies:
            copy.wait()

    def block(k):
        return held[k & 1, ((k >> 1) & (NZ - 1)) * NX + ((x - (k >> 4)) & (NX - 1))]

    for o in range(OUT_STEP):
        pair = [block(contacts[m, step * OUT_STEP + o]) for m in range(2)]
        cot = cot_ref[:, o * BS : (o + 1) * BS]
        terms = contract(jnp.concatenate(pair), cot, (1, 0)).astype(BF16)
        out_ref[2 * o : 2 * o + 2] = terms.reshape(2, BS, BS)


def out_terms(place, contacts, cotangent, own, other):
    rows = cotangent.shape[0]
    count = contacts.shape[1]
    return pl.pallas_call(
        out_kernel,
        grid_spec=pltpu.PrefetchScalarGridSpec(
            num_scalar_prefetch=2,
            grid=(count // OUT_STEP,),
            in_specs=[
                pl.BlockSpec((rows, OUT_STEP * BS), lambda g, *_: (0, g)),
                pl.BlockSpec(memory_space=pl.ANY),
                pl.BlockSpec(memory_space=pl.ANY),
            ],
            out_specs=pl.BlockSpec((2 * OUT_STEP, BS, BS), lambda g, *_: (g, 0, 0)),
            scratch_shapes=[
                pltpu.VMEM((NC, NX * NZ, BS, rows), BF16),
                pltpu.SemaphoreType.DMA((2,)),
            ],
        ),
        out_shape=jax.ShapeDtypeStruct((2 * count, BS, BS), BF16),
        compiler_params=params(56),
        cost_estimate=pl.CostEstimate(flops=3 * 10**9, bytes_accessed=2**24, transcendentals=0),
        name="out_terms",
    )(place, contacts, cotangent, own, other)


def in_kernel(place, contacts, enc_ref, *refs):
    firsts, lasts = refs[: NC * NX], refs[NC * NX : NC * NX + NC]
    send_ref, mine_ref, held, made, sems = refs[NC * NX + NC :]
    x, core, y = place[0], place[2], place[3]
    copies = []
    for n, first in enumerate(firsts):
        last = lasts[n // NX].at[:, n % NX]
        copies += [
            pltpu.make_async_copy(first, held.at[n, :, pl.ds(0, FIRST)], sems.at[n, 0]),
            pltpu.make_async_copy(last, held.at[n, :, pl.ds(FIRST, LAST)], sems.at[n, 1]),
        ]
    for copy in copies:
        copy.start()
    for copy in copies:
        copy.wait()
    per_in, count = contacts.shape
    for i in range(count):
        turned = enc_ref[:, i * BS : (i + 1) * BS].T
        for m in range(per_in):
            k = contacts[m, i]
            slot = ((k & 1) ^ core) * NX + ((x - (k >> 4)) & (NX - 1))
            made[i * per_in + m] = contract(turned, held[slot, (k >> 1) & (NZ - 1)], (1, 0))
    for n in range(count * per_in):
        send_ref[n] = made[n].astype(BF16)
    each = count * per_in // NY
    for n in range(each):
        mine_ref[n] = made[y * each + n]


def in_terms(place, contacts, encodings, parts):
    rows = encodings.shape[0]
    per_in, count = contacts.shape
    each = per_in * count // NY
    smem = pl.BlockSpec(memory_space=pltpu.SMEM)
    whole = pl.BlockSpec(memory_space=pltpu.VMEM)
    return pl.pallas_call(
        in_kernel,
        in_specs=[smem, smem, whole] + [pl.BlockSpec(memory_space=pl.ANY)] * (NC * NX + NC),
        out_specs=[whole] * 2,
        scratch_shapes=[
            pltpu.VMEM((NC * NX, NZ, rows, BS), BF16),
            pltpu.VMEM((per_in * count, BS, BS), F32),
            pltpu.SemaphoreType.DMA((NC * NX, 2)),
        ],
        out_shape=[
            jax.ShapeDtypeStruct((per_in * count, BS, BS), BF16),
            jax.ShapeDtypeStruct((each, BS, BS), F32),
        ],
        compiler_params=params(14),
        cost_estimate=pl.CostEstimate(flops=5 * 10**8, bytes_accessed=2**23, transcendentals=0),
        name="in_terms",
    )(place, contacts, encodings, *parts)


def sum_parts(parts, own, at):
    which = lax.broadcasted_iota(jnp.int32, parts.shape, 0)
    return jnp.sum(jnp.where(which == at, own[None], parts.astype(F32)), axis=0)


def silu_slope(values):
    sigma = jax.nn.sigmoid(values)
    return sigma * (1.0 + values * (1.0 - sigma))


def per_device(encodings, hidden_pre, cotangent, out_weights, out_contacts, in_contacts):
    position = lax.axis_index("blk")
    place = jnp.stack(
        [position // (NZ * NC), position // NC % NZ, position % NC, lax.axis_index("smp")]
    ).astype(jnp.int32)
    out_index, in_index = out_contacts.T, in_contacts.T
    pre = hidden_pre.astype(F32)

    activation = jax.nn.silu(pre).astype(BF16).T
    arrived = [moved(activation, dx=d) for d in range(1, NX)]

    send, keep = hidden_sums(place, out_index, cotangent, out_weights)
    along_x = jnp.stack([after(activation, send)] + arrived)
    send = after(send, along_x)
    act_own = lax.all_gather(along_x, "blk", axis_index_groups=LINES)
    act_own = act_own.reshape(NZ * NX, BS, -1)

    *by_x, by_plane, own_plane = core_sums(place, keep, moved(send, dc=1))
    from_x = [moved(by_x[d], dx=d) for d in range(1, NX)]
    from_z = lax.all_to_all(by_plane, "blk", 0, 0, axis_index_groups=LINES)
    last_own, *last_x = plane_sums(place, own_plane, from_z)
    by_z, own_z = line_sums(place, after(by_x[0], last_own), *from_x)
    got_z = lax.all_to_all(by_z, "blk", 0, 0, axis_index_groups=LINES)
    got_x = [moved(part, dx=d + 1) for d, part in enumerate(last_x)]

    act_own = after(act_own, by_z)
    terms = out_terms(place, out_index, cotangent, act_own, moved(act_own, dc=1))
    both = got_z[0, :16] + terms[0, :16]
    terms = after(terms, both)
    out_grad = lax.psum_scatter(terms, "smp", scatter_dimension=0, tiled=True)

    slope = silu_slope(pre)
    grad_act = sum_parts(got_z, after(own_z, both), place[1])
    first = (grad_act * slope[:FIRST]).astype(BF16)
    grad_act = sum((part.astype(F32) for part in got_x), last_own)
    last = (grad_act * slope[FIRST:]).astype(BF16)

    copies = jnp.broadcast_to(first, (NZ, *first.shape))
    along_z = lax.all_to_all(copies, "blk", 0, 0, axis_index_groups=LINES)
    last_x = jnp.stack([last] + [moved(last, dx=d) for d in range(1, NX)])
    own = [along_z] + [moved(along_z, dx=d) for d in range(1, NX)]
    copies = jnp.broadcast_to(last_x, (NZ, *last_x.shape))
    last_own = lax.all_to_all(copies, "blk", 0, 0, axis_index_groups=LINES)
    parts = own + [moved(part, dc=1) for part in own] + [last_own, moved(last_own, dc=1)]

    away, mine = in_terms(place, in_index, encodings, parts)
    away = away.reshape(NY, *mine.shape)
    away = lax.all_to_all(away, "smp", 0, 0)
    in_grad = sum_parts(away, mine, place[3]).astype(BF16)
    return (out_grad, in_grad)


def solution(mesh):
    in_specs = (
        P("smp", "blk"),
        P("smp", "blk"),
        P("smp", "blk"),
        P("blk", None, None),
        P("blk", None),
        P("blk", None),
    )
    out_specs = (P(("blk", "smp"), None, None), P(("blk", "smp"), None, None))
    return jax.shard_map(
        per_device, mesh=mesh, in_specs=in_specs, out_specs=out_specs, check_vma=False
    )
```

```python
import jax
import jax.numpy as jnp
from jax import lax
from jax.experimental import pallas as pl
from jax.experimental.pallas import tpu as pltpu
from jax.sharding import PartitionSpec as P

BF16 = jnp.bfloat16
F32 = jnp.float32
NX, NZ, NC, NY = 4, 8, 2, 4
BS = 128
STEP_BLOCKS = 28
OUT_STEP = 28
CORE_STEP = 2


def index_of(x, z, core):
    return ((x % NX) * NZ + z % NZ) * NC + core % NC


def moved(value, dx=0, dz=0, dc=0):
    pairs = [
        (index_of(x, z, c), index_of(x + dx, z + dz, c + dc))
        for x in range(NX)
        for z in range(NZ)
        for c in range(NC)
    ]
    return lax.ppermute(value, "blk", pairs)


def moved_smp(value, dy):
    return lax.ppermute(value, "smp", [(i, (i + dy) % NY) for i in range(NY)])


LINES = [[index_of(x, z, c) for z in range(NZ)] for x in range(NX) for c in range(NC)]


def params(mib):
    return pltpu.CompilerParams(vmem_limit_bytes=mib * 2**20)


def contract(lhs, rhs, over):
    return lax.dot_general(lhs, rhs, ((over[:1], over[1:]), ((), ())), preferred_element_type=F32)


def after(value, other):
    anywhere = pl.BlockSpec(memory_space=pl.ANY)
    other = other[(0,) * (other.ndim - 2)][:16] if other.ndim > 2 else other
    return pl.pallas_call(
        lambda *refs: None,
        in_specs=[anywhere, anywhere],
        out_specs=anywhere,
        out_shape=jax.ShapeDtypeStruct(value.shape, value.dtype),
        input_output_aliases={0: 0},
        name="after",
    )(value, other)


def hidden_kernel(place, contacts, cot_ref, weight_ref, send_ref, keep_ref, mark_ref, total):
    step = pl.program_id(0)
    core = place[2]

    @pl.when(step == 0)
    def _():
        total[...] = jnp.zeros_like(total)

    for o in range(STEP_BLOCKS):
        cot = cot_ref[:, o * BS : (o + 1) * BS]
        weights = weight_ref[2 * o : 2 * o + 2].reshape(2 * BS, BS)
        terms = contract(cot, weights, (1, 1))
        for m in range(2):
            k = contacts[m, step * STEP_BLOCKS + o]
            total[k] += terms[:, m * BS : (m + 1) * BS]

    @pl.when(step == pl.num_programs(0) - 1)
    def _():
        def write(p, carry):
            send_ref[p] = total[2 * p + 1 - core].astype(BF16)
            keep_ref[p] = total[2 * p + core]
            return carry

        lax.fori_loop(0, NX * NZ, write, 0)
        mark_ref[...] = jnp.zeros_like(mark_ref)


def hidden_sums(place, contacts, cotangent, weights):
    rows = cotangent.shape[0]
    count = NX * NZ
    steps = weights.shape[0] // (2 * STEP_BLOCKS)
    return pl.pallas_call(
        hidden_kernel,
        grid_spec=pltpu.PrefetchScalarGridSpec(
            num_scalar_prefetch=2,
            grid=(steps,),
            in_specs=[
                pl.BlockSpec((rows, STEP_BLOCKS * BS), lambda g, *_: (0, g)),
                pl.BlockSpec((2 * STEP_BLOCKS, BS, BS), lambda g, *_: (g, 0, 0)),
            ],
            out_specs=[
                pl.BlockSpec((count, rows, BS), lambda g, *_: (0, 0, 0)),
                pl.BlockSpec((count, rows, BS), lambda g, *_: (0, 0, 0)),
                pl.BlockSpec((8, BS), lambda g, *_: (0, 0)),
            ],
            scratch_shapes=[pltpu.VMEM((2 * count, rows, BS), F32)],
        ),
        out_shape=[
            jax.ShapeDtypeStruct((count, rows, BS), BF16),
            jax.ShapeDtypeStruct((count, rows, BS), F32),
            jax.ShapeDtypeStruct((8, BS), F32),
        ],
        compiler_params=params(56),
        cost_estimate=pl.CostEstimate(flops=3 * 10**9, bytes_accessed=2**24, transcendentals=0),
        name="hidden_sums",
    )(place, contacts, cotangent, weights)


def core_kernel(place, keep_ref, got_ref, *outs):
    x = place[0]
    for d in range(NX):
        at = (x + d) & (NX - 1)
        for n in range(CORE_STEP):
            outs[d][n] = (keep_ref[at, n] + got_ref[at, n].astype(F32)).astype(outs[d].dtype)


def core_sums(place, keep, got):
    rows = keep.shape[1]
    spec = pl.BlockSpec((NX, CORE_STEP, rows, BS), lambda g, *_: (0, g, 0, 0))
    return pl.pallas_call(
        core_kernel,
        grid_spec=pltpu.PrefetchScalarGridSpec(
            num_scalar_prefetch=1,
            grid=(NZ // CORE_STEP,),
            in_specs=[spec, spec],
            out_specs=[pl.BlockSpec((CORE_STEP, rows, BS), lambda g, *_: (g, 0, 0))] * NX,
        ),
        out_shape=[
            jax.ShapeDtypeStruct((NZ, rows, BS), BF16 if d else F32) for d in range(NX)
        ],
        compiler_params=params(16),
        cost_estimate=pl.CostEstimate(flops=10**6, bytes_accessed=2**23, transcendentals=0),
        name="core_sums",
    )(place, keep.reshape(NX, NZ, rows, BS), got.reshape(NX, NZ, rows, BS))


def line_kernel(place, keep_ref, a_ref, b_ref, c_ref, send_ref, own_ref):
    def total(at):
        return keep_ref[at] + a_ref[at].astype(F32) + b_ref[at].astype(F32) + c_ref[at].astype(F32)

    for at in range(NZ):
        send_ref[at] = total(at).astype(BF16)
    own_ref[...] = total(place[1])


def line_sums(place, keep, *got):
    rows = keep.shape[1]
    whole = pl.BlockSpec(memory_space=pltpu.VMEM)
    return pl.pallas_call(
        line_kernel,
        in_specs=[pl.BlockSpec(memory_space=pltpu.SMEM)] + [whole] * NX,
        out_specs=[whole] * 2,
        out_shape=[
            jax.ShapeDtypeStruct((NZ, rows, BS), BF16),
            jax.ShapeDtypeStruct((rows, BS), F32),
        ],
        compiler_params=params(8),
        cost_estimate=pl.CostEstimate(flops=10**6, bytes_accessed=2**22, transcendentals=0),
        name="line_sums",
    )(place, keep, *got)


def out_kernel(place, contacts, cot_ref, own_ref, other_ref, out_ref, held, sems):
    step = pl.program_id(0)
    x, core = place[0], place[2]

    @pl.when(step == 0)
    def _():
        copies = [
            pltpu.make_async_copy(own_ref, held.at[core], sems.at[0]),
            pltpu.make_async_copy(other_ref, held.at[1 - core], sems.at[1]),
        ]
        for copy in copies:
            copy.start()
        for copy in copies:
            copy.wait()

    def block(k):
        return held[k & 1, ((k >> 1) & (NZ - 1)) * NX + ((x - (k >> 4)) & (NX - 1))]

    for o in range(OUT_STEP):
        pair = [block(contacts[m, step * OUT_STEP + o]) for m in range(2)]
        cot = cot_ref[:, o * BS : (o + 1) * BS]
        terms = contract(jnp.concatenate(pair), cot, (1, 0)).astype(BF16)
        out_ref[2 * o : 2 * o + 2] = terms.reshape(2, BS, BS)


def out_terms(place, contacts, cotangent, own, other):
    rows = cotangent.shape[0]
    count = contacts.shape[1]
    return pl.pallas_call(
        out_kernel,
        grid_spec=pltpu.PrefetchScalarGridSpec(
            num_scalar_prefetch=2,
            grid=(count // OUT_STEP,),
            in_specs=[
                pl.BlockSpec((rows, OUT_STEP * BS), lambda g, *_: (0, g)),
                pl.BlockSpec(memory_space=pl.ANY),
                pl.BlockSpec(memory_space=pl.ANY),
            ],
            out_specs=pl.BlockSpec((2 * OUT_STEP, BS, BS), lambda g, *_: (g, 0, 0)),
            scratch_shapes=[
                pltpu.VMEM((NC, NX * NZ, BS, rows), BF16),
                pltpu.SemaphoreType.DMA((2,)),
            ],
        ),
        out_shape=jax.ShapeDtypeStruct((2 * count, BS, BS), BF16),
        compiler_params=params(56),
        cost_estimate=pl.CostEstimate(flops=3 * 10**9, bytes_accessed=2**24, transcendentals=0),
        name="out_terms",
    )(place, contacts, cotangent, own, other)


def in_kernel(place, contacts, enc_ref, *refs):
    parts, outs = refs[: NC * NX], refs[NC * NX : NC * NX + NY]
    held, made, sems = refs[NC * NX + NY :]
    x, core, y = place[0], place[2], place[3]
    copies = [
        pltpu.make_async_copy(part, held.at[n], sems.at[n]) for n, part in enumerate(parts)
    ]
    for copy in copies:
        copy.start()
    for copy in copies:
        copy.wait()
    per_in, count = contacts.shape
    for i in range(count):
        turned = enc_ref[:, i * BS : (i + 1) * BS].T
        for m in range(per_in):
            k = contacts[m, i]
            slot = ((k & 1) ^ core) * NX + ((x - (k >> 4)) & (NX - 1))
            made[i * per_in + m] = contract(turned, held[slot, (k >> 1) & (NZ - 1)], (1, 0))
    each = count * per_in // NY
    for d in range(NY):
        first = ((y + d) & (NY - 1)) * each
        for n in range(each):
            outs[d][n] = made[first + n].astype(outs[d].dtype)


def in_terms(place, contacts, encodings, parts):
    rows = encodings.shape[0]
    per_in, count = contacts.shape
    each = per_in * count // NY
    smem = pl.BlockSpec(memory_space=pltpu.SMEM)
    whole = pl.BlockSpec(memory_space=pltpu.VMEM)
    return pl.pallas_call(
        in_kernel,
        in_specs=[smem, smem, whole] + [pl.BlockSpec(memory_space=pl.ANY)] * (NC * NX),
        out_specs=[whole] * NY,
        scratch_shapes=[
            pltpu.VMEM((NC * NX, NZ, rows, BS), BF16),
            pltpu.VMEM((per_in * count, BS, BS), F32),
            pltpu.SemaphoreType.DMA((NC * NX,)),
        ],
        out_shape=[jax.ShapeDtypeStruct((each, BS, BS), BF16 if d else F32) for d in range(NY)],
        compiler_params=params(14),
        cost_estimate=pl.CostEstimate(flops=5 * 10**8, bytes_accessed=2**23, transcendentals=0),
        name="in_terms",
    )(place, contacts, encodings, *parts)


def sum_parts(parts, own, at):
    which = lax.broadcasted_iota(jnp.int32, parts.shape, 0)
    return jnp.sum(jnp.where(which == at, own[None], parts.astype(F32)), axis=0)


def silu_slope(values):
    sigma = jax.nn.sigmoid(values)
    return sigma * (1.0 + values * (1.0 - sigma))


def per_device(encodings, hidden_pre, cotangent, out_weights, out_contacts, in_contacts):
    position = lax.axis_index("blk")
    place = jnp.stack(
        [position // (NZ * NC), position // NC % NZ, position % NC, lax.axis_index("smp")]
    ).astype(jnp.int32)
    out_index, in_index = out_contacts.T, in_contacts.T
    pre = hidden_pre.astype(F32)

    activation = jax.nn.silu(pre).astype(BF16).T
    arrived = [moved(activation, dx=d) for d in range(1, NX)]

    send, keep, mark = hidden_sums(place, out_index, cotangent, out_weights)
    along_x = jnp.stack([after(activation, mark)] + arrived)
    send = after(send, along_x)
    act_own = lax.all_gather(along_x, "blk", axis_index_groups=LINES)
    act_own = act_own.reshape(NZ * NX, BS, -1)

    by_x = core_sums(place, keep, moved(send, dc=1))
    by_z, own_z = line_sums(place, by_x[0], *[moved(by_x[d], dx=d) for d in range(1, NX)])
    got = lax.all_to_all(by_z, "blk", 0, 0, axis_index_groups=LINES)
    act_own = after(act_own, own_z)
    terms = out_terms(place, out_index, cotangent, act_own, moved(act_own, dc=1))
    both = got[0, :16] + terms[0, :16]
    terms = after(terms, both)
    out_grad = lax.psum_scatter(terms, "smp", scatter_dimension=0, tiled=True)

    grad_act = sum_parts(got, after(own_z, both), place[1])
    grad_pre = (grad_act * silu_slope(pre)).astype(BF16)

    copies = jnp.broadcast_to(grad_pre, (NZ, *grad_pre.shape))
    along_z = lax.all_to_all(copies, "blk", 0, 0, axis_index_groups=LINES)
    own = [along_z] + [moved(along_z, dx=d) for d in range(1, NX)]
    parts = own + [moved(part, dc=1) for part in own]

    mine, *away = in_terms(place, in_index, encodings, parts)
    in_grad = sum((moved_smp(a, d + 1).astype(F32) for d, a in enumerate(away)), mine).astype(BF16)
    return (out_grad, in_grad)


def solution(mesh):
    in_specs = (
        P("smp", "blk"),
        P("smp", "blk"),
        P("smp", "blk"),
        P("blk", None, None),
        P("blk", None),
        P("blk", None),
    )
    out_specs = (P(("blk", "smp"), None, None), P(("blk", "smp"), None, None))
    return jax.shard_map(
        per_device, mesh=mesh, in_specs=in_specs, out_specs=out_specs, check_vma=False
    )
```

```python
import jax
import jax.numpy as jnp
from jax import lax
from jax.experimental import pallas as pl
from jax.experimental.pallas import tpu as pltpu
from jax.sharding import PartitionSpec as P

BF16 = jnp.bfloat16
F32 = jnp.float32
NX, NZ, NC, NY = 4, 8, 2, 4
BS = 128
STEP_BLOCKS = 28
OUT_STEP = 28
FIRST, LAST = 192, 64
CORE_STEP = 2


def index_of(x, z, core):
    return ((x % NX) * NZ + z % NZ) * NC + core % NC


def moved(value, dx=0, dz=0, dc=0):
    pairs = [
        (index_of(x, z, c), index_of(x + dx, z + dz, c + dc))
        for x in range(NX)
        for z in range(NZ)
        for c in range(NC)
    ]
    return lax.ppermute(value, "blk", pairs)


def moved_smp(value, dy):
    return lax.ppermute(value, "smp", [(i, (i + dy) % NY) for i in range(NY)])


LINES = [[index_of(x, z, c) for z in range(NZ)] for x in range(NX) for c in range(NC)]


def params(mib):
    return pltpu.CompilerParams(vmem_limit_bytes=mib * 2**20)


def contract(lhs, rhs, over):
    return lax.dot_general(lhs, rhs, ((over[:1], over[1:]), ((), ())), preferred_element_type=F32)


def after(value, other):
    anywhere = pl.BlockSpec(memory_space=pl.ANY)
    return pl.pallas_call(
        lambda *refs: None,
        in_specs=[anywhere, anywhere],
        out_specs=anywhere,
        out_shape=jax.ShapeDtypeStruct(value.shape, value.dtype),
        input_output_aliases={0: 0},
        name="after",
    )(value, other)


def hidden_kernel(place, contacts, cot_ref, weight_ref, before_ref, send_ref, keep_ref, total):
    del before_ref
    step = pl.program_id(0)
    core = place[2]

    @pl.when(step == 0)
    def _():
        total[...] = jnp.zeros_like(total)

    for o in range(STEP_BLOCKS):
        cot = cot_ref[:, o * BS : (o + 1) * BS]
        weights = weight_ref[2 * o : 2 * o + 2].reshape(2 * BS, BS)
        terms = contract(cot, weights, (1, 1))
        for m in range(2):
            k = contacts[m, step * STEP_BLOCKS + o]
            total[k] += terms[:, m * BS : (m + 1) * BS]

    @pl.when(step == pl.num_programs(0) - 1)
    def _():
        def write(p, carry):
            send_ref[p] = total[2 * p + 1 - core].astype(BF16)
            keep_ref[p] = total[2 * p + core]
            return carry

        lax.fori_loop(0, NX * NZ, write, 0)


def hidden_sums(place, contacts, cotangent, weights, before):
    rows = cotangent.shape[0]
    count = NX * NZ
    steps = weights.shape[0] // (2 * STEP_BLOCKS)
    return pl.pallas_call(
        hidden_kernel,
        grid_spec=pltpu.PrefetchScalarGridSpec(
            num_scalar_prefetch=2,
            grid=(steps,),
            in_specs=[
                pl.BlockSpec((rows, STEP_BLOCKS * BS), lambda g, *_: (0, g)),
                pl.BlockSpec((2 * STEP_BLOCKS, BS, BS), lambda g, *_: (g, 0, 0)),
                pl.BlockSpec(memory_space=pl.ANY),
            ],
            out_specs=[
                pl.BlockSpec((count, rows, BS), lambda g, *_: (0, 0, 0)),
                pl.BlockSpec((count, rows, BS), lambda g, *_: (0, 0, 0)),
            ],
            scratch_shapes=[pltpu.VMEM((2 * count, rows, BS), F32)],
        ),
        out_shape=[
            jax.ShapeDtypeStruct((count, rows, BS), BF16),
            jax.ShapeDtypeStruct((count, rows, BS), F32),
        ],
        compiler_params=params(56),
        cost_estimate=pl.CostEstimate(flops=3 * 10**9, bytes_accessed=2**24, transcendentals=0),
        name="hidden_sums",
    )(place, contacts, cotangent, weights, before)


def core_kernel(place, keep_ref, got_ref, *outs):
    x = place[0]
    for d in range(NX):
        at = (x + d) & (NX - 1)
        for n in range(CORE_STEP):
            outs[d][n] = (keep_ref[at, n] + got_ref[at, n].astype(F32)).astype(outs[d].dtype)


def core_sums(place, keep, got):
    rows = keep.shape[1]
    spec = pl.BlockSpec((NX, CORE_STEP, rows, BS), lambda g, *_: (0, g, 0, 0))
    return pl.pallas_call(
        core_kernel,
        grid_spec=pltpu.PrefetchScalarGridSpec(
            num_scalar_prefetch=1,
            grid=(NZ // CORE_STEP,),
            in_specs=[spec, spec],
            out_specs=[pl.BlockSpec((CORE_STEP, rows, BS), lambda g, *_: (g, 0, 0))] * NX,
        ),
        out_shape=[
            jax.ShapeDtypeStruct((NZ, rows, BS), BF16 if d else F32) for d in range(NX)
        ],
        compiler_params=params(16),
        cost_estimate=pl.CostEstimate(flops=10**6, bytes_accessed=2**23, transcendentals=0),
        name="core_sums",
    )(place, keep.reshape(NX, NZ, rows, BS), got.reshape(NX, NZ, rows, BS))


def line_kernel(place, keep_ref, a_ref, b_ref, c_ref, send_ref, own_ref):
    def total(at):
        return keep_ref[at] + a_ref[at].astype(F32) + b_ref[at].astype(F32) + c_ref[at].astype(F32)

    for at in range(NZ):
        send_ref[at] = total(at).astype(BF16)
    own_ref[...] = total(place[1])


def line_sums(place, keep, *got):
    rows = keep.shape[1]
    whole = pl.BlockSpec(memory_space=pltpu.VMEM)
    return pl.pallas_call(
        line_kernel,
        in_specs=[pl.BlockSpec(memory_space=pltpu.SMEM)] + [whole] * NX,
        out_specs=[whole] * 2,
        out_shape=[
            jax.ShapeDtypeStruct((NZ, rows, BS), BF16),
            jax.ShapeDtypeStruct((rows, BS), F32),
        ],
        compiler_params=params(8),
        cost_estimate=pl.CostEstimate(flops=10**6, bytes_accessed=2**22, transcendentals=0),
        name="line_sums",
    )(place, keep, *got)


def out_kernel(place, contacts, cot_ref, own_ref, other_ref, out_ref, mark_ref, held, sems):
    step = pl.program_id(0)
    x, core = place[0], place[2]

    @pl.when(step == 0)
    def _():
        copies = [
            pltpu.make_async_copy(own_ref, held.at[core], sems.at[0]),
            pltpu.make_async_copy(other_ref, held.at[1 - core], sems.at[1]),
        ]
        for copy in copies:
            copy.start()
        for copy in copies:
            copy.wait()
        mark_ref[...] = jnp.zeros_like(mark_ref)

    def block(k):
        return held[k & 1, ((k >> 1) & (NZ - 1)) * NX + ((x - (k >> 4)) & (NX - 1))]

    for o in range(OUT_STEP):
        pair = [block(contacts[m, step * OUT_STEP + o]) for m in range(2)]
        cot = cot_ref[:, o * BS : (o + 1) * BS]
        terms = contract(jnp.concatenate(pair), cot, (1, 0)).astype(BF16)
        out_ref[2 * o : 2 * o + 2] = terms.reshape(2, BS, BS)


def out_terms(place, contacts, cotangent, own, other):
    rows = cotangent.shape[0]
    count = contacts.shape[1]
    return pl.pallas_call(
        out_kernel,
        grid_spec=pltpu.PrefetchScalarGridSpec(
            num_scalar_prefetch=2,
            grid=(count // OUT_STEP,),
            in_specs=[
                pl.BlockSpec((rows, OUT_STEP * BS), lambda g, *_: (0, g)),
                pl.BlockSpec(memory_space=pl.ANY),
                pl.BlockSpec(memory_space=pl.ANY),
            ],
            out_specs=[
                pl.BlockSpec((2 * OUT_STEP, BS, BS), lambda g, *_: (g, 0, 0)),
                pl.BlockSpec((8, BS), lambda g, *_: (0, 0)),
            ],
            scratch_shapes=[
                pltpu.VMEM((NC, NX * NZ, BS, rows), BF16),
                pltpu.SemaphoreType.DMA((2,)),
            ],
        ),
        out_shape=[
            jax.ShapeDtypeStruct((2 * count, BS, BS), BF16),
            jax.ShapeDtypeStruct((8, BS), F32),
        ],
        compiler_params=params(56),
        cost_estimate=pl.CostEstimate(flops=3 * 10**9, bytes_accessed=2**24, transcendentals=0),
        name="out_terms",
    )(place, contacts, cotangent, own, other)


def in_kernel(place, contacts, enc_ref, *refs):
    firsts, lasts = refs[: NC * NX], refs[NC * NX : NC * NX + NC]
    outs, (held, made, sems) = refs[NC * NX + NC :][:NY], refs[NC * NX + NC + NY :]
    x, core, y = place[0], place[2], place[3]
    copies = []
    for n, first in enumerate(firsts):
        last = lasts[n // NX].at[:, n % NX]
        copies += [
            pltpu.make_async_copy(first, held.at[n, :, pl.ds(0, FIRST)], sems.at[n, 0]),
            pltpu.make_async_copy(last, held.at[n, :, pl.ds(FIRST, LAST)], sems.at[n, 1]),
        ]
    for copy in copies:
        copy.start()
    for copy in copies:
        copy.wait()
    per_in, count = contacts.shape
    for i in range(count):
        turned = enc_ref[:, i * BS : (i + 1) * BS].T
        for m in range(per_in):
            k = contacts[m, i]
            slot = ((k & 1) ^ core) * NX + ((x - (k >> 4)) & (NX - 1))
            made[i * per_in + m] = contract(turned, held[slot, (k >> 1) & (NZ - 1)], (1, 0))
    each = count * per_in // NY
    for d in range(NY):
        first = ((y + d) & (NY - 1)) * each
        for n in range(each):
            outs[d][n] = made[first + n].astype(outs[d].dtype)


def in_terms(place, contacts, encodings, parts):
    rows = encodings.shape[0]
    per_in, count = contacts.shape
    each = per_in * count // NY
    smem = pl.BlockSpec(memory_space=pltpu.SMEM)
    whole = pl.BlockSpec(memory_space=pltpu.VMEM)
    return pl.pallas_call(
        in_kernel,
        in_specs=[smem, smem, whole] + [pl.BlockSpec(memory_space=pl.ANY)] * (NC * NX + NC),
        out_specs=[whole] * NY,
        scratch_shapes=[
            pltpu.VMEM((NC * NX, NZ, rows, BS), BF16),
            pltpu.VMEM((per_in * count, BS, BS), F32),
            pltpu.SemaphoreType.DMA((NC * NX, 2)),
        ],
        out_shape=[jax.ShapeDtypeStruct((each, BS, BS), BF16 if d else F32) for d in range(NY)],
        compiler_params=params(14),
        cost_estimate=pl.CostEstimate(flops=5 * 10**8, bytes_accessed=2**23, transcendentals=0),
        name="in_terms",
    )(place, contacts, encodings, *parts)


def sum_parts(parts, own, at):
    which = lax.broadcasted_iota(jnp.int32, parts.shape, 0)
    return jnp.sum(jnp.where(which == at, own[None], parts.astype(F32)), axis=0)


def silu_slope(values):
    sigma = jax.nn.sigmoid(values)
    return sigma * (1.0 + values * (1.0 - sigma))


def per_device(encodings, hidden_pre, cotangent, out_weights, out_contacts, in_contacts):
    position = lax.axis_index("blk")
    place = jnp.stack(
        [position // (NZ * NC), position // NC % NZ, position % NC, lax.axis_index("smp")]
    ).astype(jnp.int32)
    out_index, in_index = out_contacts.T, in_contacts.T
    pre = hidden_pre.astype(F32)

    activation = jax.nn.silu(pre).astype(BF16).T
    along_x = jnp.stack([activation] + [moved(activation, dx=d) for d in range(1, NX)])
    act_own = lax.all_gather(along_x, "blk", axis_index_groups=LINES)
    act_own = act_own.reshape(NZ * NX, BS, -1)
    send, keep = hidden_sums(place, out_index, cotangent, out_weights, along_x)

    by_x = core_sums(place, keep, moved(send, dc=1))
    by_z, own_z = line_sums(place, by_x[0], *[moved(by_x[d], dx=d) for d in range(1, NX)])
    got = lax.all_to_all(by_z, "blk", 0, 0, axis_index_groups=LINES)

    act_own = after(act_own, own_z)
    terms, done = out_terms(place, out_index, cotangent, act_own, moved(act_own, dc=1))
    grad_act = sum_parts(got, after(own_z, done), place[1])
    slope = silu_slope(pre)
    first = (grad_act[:FIRST] * slope[:FIRST]).astype(BF16)
    last = (grad_act[FIRST:] * slope[FIRST:]).astype(BF16)
    out_grad = lax.psum_scatter(after(terms, first), "smp", scatter_dimension=0, tiled=True)

    last_x = jnp.stack([last] + [moved(last, dx=d) for d in range(1, NX)])
    copies = jnp.broadcast_to(first, (NZ, *first.shape))
    along_z = lax.all_to_all(copies, "blk", 0, 0, axis_index_groups=LINES)
    own = [along_z] + [moved(along_z, dx=d) for d in range(1, NX)]
    copies = jnp.broadcast_to(last_x, (NZ, *last_x.shape))
    last_own = lax.all_to_all(copies, "blk", 0, 0, axis_index_groups=LINES)
    parts = own + [moved(part, dc=1) for part in own] + [last_own, moved(last_own, dc=1)]

    mine, *away = in_terms(place, in_index, encodings, parts)
    in_grad = sum((moved_smp(a, d + 1).astype(F32) for d, a in enumerate(away)), mine).astype(BF16)
    return (out_grad, in_grad)


def solution(mesh):
    in_specs = (
        P("smp", "blk"),
        P("smp", "blk"),
        P("smp", "blk"),
        P("blk", None, None),
        P("blk", None),
        P("blk", None),
    )
    out_specs = (P(("blk", "smp"), None, None), P(("blk", "smp"), None, None))
    return jax.shard_map(
        per_device, mesh=mesh, in_specs=in_specs, out_specs=out_specs, check_vma=False
    )
```

```python
import jax
import jax.numpy as jnp
from jax import lax
from jax.experimental import pallas as pl
from jax.experimental.pallas import tpu as pltpu
from jax.sharding import PartitionSpec as P

BF16 = jnp.bfloat16
F32 = jnp.float32
NX, NZ, NC, NY = 4, 8, 2, 4
BS = 128
STEP_BLOCKS = 28
OUT_STEP = 28
FIRST, LAST = 208, 48
CORE_STEP = 2


def index_of(x, z, core):
    return ((x % NX) * NZ + z % NZ) * NC + core % NC


def moved(value, dx=0, dz=0, dc=0):
    pairs = [
        (index_of(x, z, c), index_of(x + dx, z + dz, c + dc))
        for x in range(NX)
        for z in range(NZ)
        for c in range(NC)
    ]
    return lax.ppermute(value, "blk", pairs)


def moved_smp(value, dy):
    return lax.ppermute(value, "smp", [(i, (i + dy) % NY) for i in range(NY)])


LINES = [[index_of(x, z, c) for z in range(NZ)] for x in range(NX) for c in range(NC)]


def params(mib):
    return pltpu.CompilerParams(vmem_limit_bytes=mib * 2**20)


def contract(lhs, rhs, over):
    return lax.dot_general(lhs, rhs, ((over[:1], over[1:]), ((), ())), preferred_element_type=F32)


def after(value, other, mib=56):
    anywhere = pl.BlockSpec(memory_space=pl.ANY)
    return pl.pallas_call(
        lambda *refs: None,
        in_specs=[anywhere, anywhere],
        out_specs=anywhere,
        out_shape=jax.ShapeDtypeStruct(value.shape, value.dtype),
        input_output_aliases={0: 0},
        name="after",
    )(value, other)


def hidden_kernel(place, contacts, cot_ref, weight_ref, before_ref, send_ref, keep_ref, total):
    del before_ref
    step = pl.program_id(0)
    core = place[2]

    @pl.when(step == 0)
    def _():
        total[...] = jnp.zeros_like(total)

    for o in range(STEP_BLOCKS):
        cot = cot_ref[:, o * BS : (o + 1) * BS]
        weights = weight_ref[2 * o : 2 * o + 2].reshape(2 * BS, BS)
        terms = contract(cot, weights, (1, 1))
        for m in range(2):
            k = contacts[m, step * STEP_BLOCKS + o]
            total[k] += terms[:, m * BS : (m + 1) * BS]

    @pl.when(step == pl.num_programs(0) - 1)
    def _():
        def write(p, carry):
            send_ref[p] = total[2 * p + 1 - core].astype(BF16)
            keep_ref[p] = total[2 * p + core]
            return carry

        lax.fori_loop(0, NX * NZ, write, 0)


def hidden_sums(place, contacts, cotangent, weights, before):
    rows = cotangent.shape[0]
    count = NX * NZ
    steps = weights.shape[0] // (2 * STEP_BLOCKS)
    return pl.pallas_call(
        hidden_kernel,
        grid_spec=pltpu.PrefetchScalarGridSpec(
            num_scalar_prefetch=2,
            grid=(steps,),
            in_specs=[
                pl.BlockSpec((rows, STEP_BLOCKS * BS), lambda g, *_: (0, g)),
                pl.BlockSpec((2 * STEP_BLOCKS, BS, BS), lambda g, *_: (g, 0, 0)),
                pl.BlockSpec(memory_space=pl.ANY),
            ],
            out_specs=[
                pl.BlockSpec((count, rows, BS), lambda g, *_: (0, 0, 0)),
                pl.BlockSpec((count, rows, BS), lambda g, *_: (0, 0, 0)),
            ],
            scratch_shapes=[pltpu.VMEM((2 * count, rows, BS), F32)],
        ),
        out_shape=[
            jax.ShapeDtypeStruct((count, rows, BS), BF16),
            jax.ShapeDtypeStruct((count, rows, BS), F32),
        ],
        compiler_params=params(44),
        cost_estimate=pl.CostEstimate(flops=3 * 10**9, bytes_accessed=2**24, transcendentals=0),
        name="hidden_sums",
    )(place, contacts, cotangent, weights, before)


def core_kernel(place, keep_ref, got_ref, *outs):
    x = place[0]
    for d in range(NX):
        at = (x + d) & (NX - 1)
        for n in range(CORE_STEP):
            outs[d][n] = (keep_ref[at, n] + got_ref[at, n].astype(F32)).astype(outs[d].dtype)


def core_sums(place, keep, got):
    rows = keep.shape[1]
    spec = pl.BlockSpec((NX, CORE_STEP, rows, BS), lambda g, *_: (0, g, 0, 0))
    return pl.pallas_call(
        core_kernel,
        grid_spec=pltpu.PrefetchScalarGridSpec(
            num_scalar_prefetch=1,
            grid=(NZ // CORE_STEP,),
            in_specs=[spec, spec],
            out_specs=[pl.BlockSpec((CORE_STEP, rows, BS), lambda g, *_: (g, 0, 0))] * NX,
        ),
        out_shape=[
            jax.ShapeDtypeStruct((NZ, rows, BS), BF16 if d else F32) for d in range(NX)
        ],
        compiler_params=params(16),
        cost_estimate=pl.CostEstimate(flops=10**6, bytes_accessed=2**23, transcendentals=0),
        name="core_sums",
    )(place, keep.reshape(NX, NZ, rows, BS), got.reshape(NX, NZ, rows, BS))


def line_kernel(place, keep_ref, a_ref, b_ref, c_ref, send_ref, own_ref):
    def total(at):
        return keep_ref[at] + a_ref[at].astype(F32) + b_ref[at].astype(F32) + c_ref[at].astype(F32)

    for at in range(NZ):
        send_ref[at] = total(at).astype(BF16)
    own_ref[...] = total(place[1])


def line_sums(place, keep, *got):
    rows = keep.shape[1]
    whole = pl.BlockSpec(memory_space=pltpu.VMEM)
    return pl.pallas_call(
        line_kernel,
        in_specs=[pl.BlockSpec(memory_space=pltpu.SMEM)] + [whole] * NX,
        out_specs=[whole] * 2,
        out_shape=[
            jax.ShapeDtypeStruct((NZ, rows, BS), BF16),
            jax.ShapeDtypeStruct((rows, BS), F32),
        ],
        compiler_params=params(8),
        cost_estimate=pl.CostEstimate(flops=10**6, bytes_accessed=2**22, transcendentals=0),
        name="line_sums",
    )(place, keep, *got)


def out_kernel(place, contacts, cot_ref, own_ref, other_ref, out_ref, mark_ref, held, sems):
    step = pl.program_id(0)
    x, core = place[0], place[2]

    @pl.when(step == 0)
    def _():
        copies = [
            pltpu.make_async_copy(own_ref, held.at[core], sems.at[0]),
            pltpu.make_async_copy(other_ref, held.at[1 - core], sems.at[1]),
        ]
        for copy in copies:
            copy.start()
        for copy in copies:
            copy.wait()
        mark_ref[...] = jnp.zeros_like(mark_ref)

    def block(k):
        return held[k & 1, ((k >> 1) & (NZ - 1)) * NX + ((x - (k >> 4)) & (NX - 1))]

    for o in range(OUT_STEP):
        pair = [block(contacts[m, step * OUT_STEP + o]) for m in range(2)]
        cot = cot_ref[:, o * BS : (o + 1) * BS]
        terms = contract(jnp.concatenate(pair), cot, (1, 0)).astype(BF16)
        out_ref[2 * o : 2 * o + 2] = terms.reshape(2, BS, BS)


def out_terms(place, contacts, cotangent, own, other):
    rows = cotangent.shape[0]
    count = contacts.shape[1]
    return pl.pallas_call(
        out_kernel,
        grid_spec=pltpu.PrefetchScalarGridSpec(
            num_scalar_prefetch=2,
            grid=(count // OUT_STEP,),
            in_specs=[
                pl.BlockSpec((rows, OUT_STEP * BS), lambda g, *_: (0, g)),
                pl.BlockSpec(memory_space=pl.ANY),
                pl.BlockSpec(memory_space=pl.ANY),
            ],
            out_specs=[
                pl.BlockSpec((2 * OUT_STEP, BS, BS), lambda g, *_: (g, 0, 0)),
                pl.BlockSpec((8, BS), lambda g, *_: (0, 0)),
            ],
            scratch_shapes=[
                pltpu.VMEM((NC, NX * NZ, BS, rows), BF16),
                pltpu.SemaphoreType.DMA((2,)),
            ],
        ),
        out_shape=[
            jax.ShapeDtypeStruct((2 * count, BS, BS), BF16),
            jax.ShapeDtypeStruct((8, BS), F32),
        ],
        compiler_params=params(48),
        cost_estimate=pl.CostEstimate(flops=3 * 10**9, bytes_accessed=2**24, transcendentals=0),
        name="out_terms",
    )(place, contacts, cotangent, own, other)


def in_kernel(place, contacts, enc_ref, *refs):
    firsts, lasts = refs[: NC * NX], refs[NC * NX : NC * NX + NC]
    outs, (held, made, sems) = refs[NC * NX + NC :][:NY], refs[NC * NX + NC + NY :]
    x, core, y = place[0], place[2], place[3]
    copies = []
    for n, first in enumerate(firsts):
        last = lasts[n // NX].at[:, n % NX]
        copies += [
            pltpu.make_async_copy(first, held.at[n, :, pl.ds(0, FIRST)], sems.at[n, 0]),
            pltpu.make_async_copy(last, held.at[n, :, pl.ds(FIRST, LAST)], sems.at[n, 1]),
        ]
    for copy in copies:
        copy.start()
    for copy in copies:
        copy.wait()
    per_in, count = contacts.shape
    for i in range(count):
        turned = enc_ref[:, i * BS : (i + 1) * BS].T
        for m in range(per_in):
            k = contacts[m, i]
            slot = ((k & 1) ^ core) * NX + ((x - (k >> 4)) & (NX - 1))
            made[i * per_in + m] = contract(turned, held[slot, (k >> 1) & (NZ - 1)], (1, 0))
    each = count * per_in // NY
    for d in range(NY):
        first = ((y + d) & (NY - 1)) * each
        for n in range(each):
            outs[d][n] = made[first + n].astype(outs[d].dtype)


def in_terms(place, contacts, encodings, parts):
    rows = encodings.shape[0]
    per_in, count = contacts.shape
    each = per_in * count // NY
    smem = pl.BlockSpec(memory_space=pltpu.SMEM)
    whole = pl.BlockSpec(memory_space=pltpu.VMEM)
    return pl.pallas_call(
        in_kernel,
        in_specs=[smem, smem, whole] + [pl.BlockSpec(memory_space=pl.ANY)] * (NC * NX + NC),
        out_specs=[whole] * NY,
        scratch_shapes=[
            pltpu.VMEM((NC * NX, NZ, rows, BS), BF16),
            pltpu.VMEM((per_in * count, BS, BS), F32),
            pltpu.SemaphoreType.DMA((NC * NX, 2)),
        ],
        out_shape=[jax.ShapeDtypeStruct((each, BS, BS), BF16 if d else F32) for d in range(NY)],
        compiler_params=params(14),
        cost_estimate=pl.CostEstimate(flops=5 * 10**8, bytes_accessed=2**23, transcendentals=0),
        name="in_terms",
    )(place, contacts, encodings, *parts)


def sum_parts(parts, own, at):
    which = lax.broadcasted_iota(jnp.int32, parts.shape, 0)
    return jnp.sum(jnp.where(which == at, own[None], parts.astype(F32)), axis=0)


def silu_slope(values):
    sigma = jax.nn.sigmoid(values)
    return sigma * (1.0 + values * (1.0 - sigma))


def per_device(encodings, hidden_pre, cotangent, out_weights, out_contacts, in_contacts):
    position = lax.axis_index("blk")
    place = jnp.stack(
        [position // (NZ * NC), position // NC % NZ, position % NC, lax.axis_index("smp")]
    ).astype(jnp.int32)
    out_index, in_index = out_contacts.T, in_contacts.T
    pre = hidden_pre.astype(F32)

    activation = jax.nn.silu(pre).astype(BF16).T
    along_x = jnp.stack([activation] + [moved(activation, dx=d) for d in range(1, NX)])
    act_own = lax.all_gather(along_x, "blk", axis_index_groups=LINES)
    act_own = act_own.reshape(NZ * NX, BS, -1)
    send, keep = hidden_sums(place, out_index, cotangent, out_weights, along_x)

    by_x = core_sums(place, keep, moved(send, dc=1))
    by_z, own_z = line_sums(place, by_x[0], *[moved(by_x[d], dx=d) for d in range(1, NX)])
    got = lax.all_to_all(by_z, "blk", 0, 0, axis_index_groups=LINES)

    act_own = after(act_own, own_z)
    terms, done = out_terms(place, out_index, cotangent, act_own, moved(act_own, dc=1))
    grad_act = sum_parts(got, after(own_z, done), place[1])
    slope = silu_slope(pre)
    first = (grad_act[:FIRST] * slope[:FIRST]).astype(BF16)
    last = (grad_act[FIRST:] * slope[FIRST:]).astype(BF16)
    out_grad = lax.psum_scatter(after(terms, first), "smp", scatter_dimension=0, tiled=True)

    last_x = jnp.stack([last] + [moved(last, dx=d) for d in range(1, NX)])
    copies = jnp.broadcast_to(first, (NZ, *first.shape))
    along_z = lax.all_to_all(copies, "blk", 0, 0, axis_index_groups=LINES)
    own = [along_z] + [moved(along_z, dx=d) for d in range(1, NX)]
    copies = jnp.broadcast_to(last_x, (NZ, *last_x.shape))
    last_own = lax.all_to_all(copies, "blk", 0, 0, axis_index_groups=LINES)
    parts = own + [moved(part, dc=1) for part in own] + [last_own, moved(last_own, dc=1)]

    mine, *away = in_terms(place, in_index, encodings, parts)
    in_grad = sum((moved_smp(a, d + 1).astype(F32) for d, a in enumerate(away)), mine).astype(BF16)
    return (out_grad, in_grad)


def solution(mesh):
    in_specs = (
        P("smp", "blk"),
        P("smp", "blk"),
        P("smp", "blk"),
        P("blk", None, None),
        P("blk", None),
        P("blk", None),
    )
    out_specs = (P(("blk", "smp"), None, None), P(("blk", "smp"), None, None))
    return jax.shard_map(
        per_device, mesh=mesh, in_specs=in_specs, out_specs=out_specs, check_vma=False
    )
```

```python
import jax
import jax.numpy as jnp
from jax import lax
from jax.experimental import pallas as pl
from jax.experimental.pallas import tpu as pltpu
from jax.sharding import PartitionSpec as P

BF16 = jnp.bfloat16
F32 = jnp.float32
NX, NZ, NC, NY = 4, 8, 2, 4
BS = 128
STEP_BLOCKS = 28
OUT_STEP = 28
FIRST, LAST = 176, 80
CORE_STEP = 2


def index_of(x, z, core):
    return ((x % NX) * NZ + z % NZ) * NC + core % NC


def moved(value, dx=0, dz=0, dc=0):
    pairs = [
        (index_of(x, z, c), index_of(x + dx, z + dz, c + dc))
        for x in range(NX)
        for z in range(NZ)
        for c in range(NC)
    ]
    return lax.ppermute(value, "blk", pairs)


def moved_smp(value, dy):
    return lax.ppermute(value, "smp", [(i, (i + dy) % NY) for i in range(NY)])


LINES = [[index_of(x, z, c) for z in range(NZ)] for x in range(NX) for c in range(NC)]


def params(mib):
    return pltpu.CompilerParams(vmem_limit_bytes=mib * 2**20)


def contract(lhs, rhs, over):
    return lax.dot_general(lhs, rhs, ((over[:1], over[1:]), ((), ())), preferred_element_type=F32)


def after(value, other, mib=56):
    anywhere = pl.BlockSpec(memory_space=pl.ANY)
    return pl.pallas_call(
        lambda *refs: None,
        in_specs=[anywhere, anywhere],
        out_specs=anywhere,
        out_shape=jax.ShapeDtypeStruct(value.shape, value.dtype),
        input_output_aliases={0: 0},
        name="after",
    )(value, other)


def hidden_kernel(place, contacts, cot_ref, weight_ref, before_ref, send_ref, keep_ref, total):
    del before_ref
    step = pl.program_id(0)
    core = place[2]

    @pl.when(step == 0)
    def _():
        total[...] = jnp.zeros_like(total)

    for o in range(STEP_BLOCKS):
        cot = cot_ref[:, o * BS : (o + 1) * BS]
        weights = weight_ref[2 * o : 2 * o + 2].reshape(2 * BS, BS)
        terms = contract(cot, weights, (1, 1))
        for m in range(2):
            k = contacts[m, step * STEP_BLOCKS + o]
            total[k] += terms[:, m * BS : (m + 1) * BS]

    @pl.when(step == pl.num_programs(0) - 1)
    def _():
        def write(p, carry):
            send_ref[p] = total[2 * p + 1 - core].astype(BF16)
            keep_ref[p] = total[2 * p + core]
            return carry

        lax.fori_loop(0, NX * NZ, write, 0)


def hidden_sums(place, contacts, cotangent, weights, before):
    rows = cotangent.shape[0]
    count = NX * NZ
    steps = weights.shape[0] // (2 * STEP_BLOCKS)
    return pl.pallas_call(
        hidden_kernel,
        grid_spec=pltpu.PrefetchScalarGridSpec(
            num_scalar_prefetch=2,
            grid=(steps,),
            in_specs=[
                pl.BlockSpec((rows, STEP_BLOCKS * BS), lambda g, *_: (0, g)),
                pl.BlockSpec((2 * STEP_BLOCKS, BS, BS), lambda g, *_: (g, 0, 0)),
                pl.BlockSpec(memory_space=pl.ANY),
            ],
            out_specs=[
                pl.BlockSpec((count, rows, BS), lambda g, *_: (0, 0, 0)),
                pl.BlockSpec((count, rows, BS), lambda g, *_: (0, 0, 0)),
            ],
            scratch_shapes=[pltpu.VMEM((2 * count, rows, BS), F32)],
        ),
        out_shape=[
            jax.ShapeDtypeStruct((count, rows, BS), BF16),
            jax.ShapeDtypeStruct((count, rows, BS), F32),
        ],
        compiler_params=params(44),
        cost_estimate=pl.CostEstimate(flops=3 * 10**9, bytes_accessed=2**24, transcendentals=0),
        name="hidden_sums",
    )(place, contacts, cotangent, weights, before)


def core_kernel(place, keep_ref, got_ref, *outs):
    x = place[0]
    for d in range(NX):
        at = (x + d) & (NX - 1)
        for n in range(CORE_STEP):
            outs[d][n] = (keep_ref[at, n] + got_ref[at, n].astype(F32)).astype(outs[d].dtype)


def core_sums(place, keep, got):
    rows = keep.shape[1]
    spec = pl.BlockSpec((NX, CORE_STEP, rows, BS), lambda g, *_: (0, g, 0, 0))
    return pl.pallas_call(
        core_kernel,
        grid_spec=pltpu.PrefetchScalarGridSpec(
            num_scalar_prefetch=1,
            grid=(NZ // CORE_STEP,),
            in_specs=[spec, spec],
            out_specs=[pl.BlockSpec((CORE_STEP, rows, BS), lambda g, *_: (g, 0, 0))] * NX,
        ),
        out_shape=[
            jax.ShapeDtypeStruct((NZ, rows, BS), BF16 if d else F32) for d in range(NX)
        ],
        compiler_params=params(16),
        cost_estimate=pl.CostEstimate(flops=10**6, bytes_accessed=2**23, transcendentals=0),
        name="core_sums",
    )(place, keep.reshape(NX, NZ, rows, BS), got.reshape(NX, NZ, rows, BS))


def line_kernel(place, keep_ref, a_ref, b_ref, c_ref, send_ref, own_ref):
    def total(at):
        return keep_ref[at] + a_ref[at].astype(F32) + b_ref[at].astype(F32) + c_ref[at].astype(F32)

    for at in range(NZ):
        send_ref[at] = total(at).astype(BF16)
    own_ref[...] = total(place[1])


def line_sums(place, keep, *got):
    rows = keep.shape[1]
    whole = pl.BlockSpec(memory_space=pltpu.VMEM)
    return pl.pallas_call(
        line_kernel,
        in_specs=[pl.BlockSpec(memory_space=pltpu.SMEM)] + [whole] * NX,
        out_specs=[whole] * 2,
        out_shape=[
            jax.ShapeDtypeStruct((NZ, rows, BS), BF16),
            jax.ShapeDtypeStruct((rows, BS), F32),
        ],
        compiler_params=params(8),
        cost_estimate=pl.CostEstimate(flops=10**6, bytes_accessed=2**22, transcendentals=0),
        name="line_sums",
    )(place, keep, *got)


def out_kernel(place, contacts, cot_ref, own_ref, other_ref, out_ref, mark_ref, held, sems):
    step = pl.program_id(0)
    x, core = place[0], place[2]

    @pl.when(step == 0)
    def _():
        copies = [
            pltpu.make_async_copy(own_ref, held.at[core], sems.at[0]),
            pltpu.make_async_copy(other_ref, held.at[1 - core], sems.at[1]),
        ]
        for copy in copies:
            copy.start()
        for copy in copies:
            copy.wait()
        mark_ref[...] = jnp.zeros_like(mark_ref)

    def block(k):
        return held[k & 1, ((k >> 1) & (NZ - 1)) * NX + ((x - (k >> 4)) & (NX - 1))]

    for o in range(OUT_STEP):
        pair = [block(contacts[m, step * OUT_STEP + o]) for m in range(2)]
        cot = cot_ref[:, o * BS : (o + 1) * BS]
        terms = contract(jnp.concatenate(pair), cot, (1, 0)).astype(BF16)
        out_ref[2 * o : 2 * o + 2] = terms.reshape(2, BS, BS)


def out_terms(place, contacts, cotangent, own, other):
    rows = cotangent.shape[0]
    count = contacts.shape[1]
    return pl.pallas_call(
        out_kernel,
        grid_spec=pltpu.PrefetchScalarGridSpec(
            num_scalar_prefetch=2,
            grid=(count // OUT_STEP,),
            in_specs=[
                pl.BlockSpec((rows, OUT_STEP * BS), lambda g, *_: (0, g)),
                pl.BlockSpec(memory_space=pl.ANY),
                pl.BlockSpec(memory_space=pl.ANY),
            ],
            out_specs=[
                pl.BlockSpec((2 * OUT_STEP, BS, BS), lambda g, *_: (g, 0, 0)),
                pl.BlockSpec((8, BS), lambda g, *_: (0, 0)),
            ],
            scratch_shapes=[
                pltpu.VMEM((NC, NX * NZ, BS, rows), BF16),
                pltpu.SemaphoreType.DMA((2,)),
            ],
        ),
        out_shape=[
            jax.ShapeDtypeStruct((2 * count, BS, BS), BF16),
            jax.ShapeDtypeStruct((8, BS), F32),
        ],
        compiler_params=params(48),
        cost_estimate=pl.CostEstimate(flops=3 * 10**9, bytes_accessed=2**24, transcendentals=0),
        name="out_terms",
    )(place, contacts, cotangent, own, other)


def in_kernel(place, contacts, enc_ref, *refs):
    firsts, lasts = refs[: NC * NX], refs[NC * NX : NC * NX + NC]
    outs, (held, made, sems) = refs[NC * NX + NC :][:NY], refs[NC * NX + NC + NY :]
    x, core, y = place[0], place[2], place[3]
    copies = []
    for n, first in enumerate(firsts):
        last = lasts[n // NX].at[:, n % NX]
        copies += [
            pltpu.make_async_copy(first, held.at[n, :, pl.ds(0, FIRST)], sems.at[n, 0]),
            pltpu.make_async_copy(last, held.at[n, :, pl.ds(FIRST, LAST)], sems.at[n, 1]),
        ]
    for copy in copies:
        copy.start()
    for copy in copies:
        copy.wait()
    per_in, count = contacts.shape
    for i in range(count):
        turned = enc_ref[:, i * BS : (i + 1) * BS].T
        for m in range(per_in):
            k = contacts[m, i]
            slot = ((k & 1) ^ core) * NX + ((x - (k >> 4)) & (NX - 1))
            made[i * per_in + m] = contract(turned, held[slot, (k >> 1) & (NZ - 1)], (1, 0))
    each = count * per_in // NY
    for d in range(NY):
        first = ((y + d) & (NY - 1)) * each
        for n in range(each):
            outs[d][n] = made[first + n].astype(outs[d].dtype)


def in_terms(place, contacts, encodings, parts):
    rows = encodings.shape[0]
    per_in, count = contacts.shape
    each = per_in * count // NY
    smem = pl.BlockSpec(memory_space=pltpu.SMEM)
    whole = pl.BlockSpec(memory_space=pltpu.VMEM)
    return pl.pallas_call(
        in_kernel,
        in_specs=[smem, smem, whole] + [pl.BlockSpec(memory_space=pl.ANY)] * (NC * NX + NC),
        out_specs=[whole] * NY,
        scratch_shapes=[
            pltpu.VMEM((NC * NX, NZ, rows, BS), BF16),
            pltpu.VMEM((per_in * count, BS, BS), F32),
            pltpu.SemaphoreType.DMA((NC * NX, 2)),
        ],
        out_shape=[jax.ShapeDtypeStruct((each, BS, BS), BF16 if d else F32) for d in range(NY)],
        compiler_params=params(14),
        cost_estimate=pl.CostEstimate(flops=5 * 10**8, bytes_accessed=2**23, transcendentals=0),
        name="in_terms",
    )(place, contacts, encodings, *parts)


def sum_parts(parts, own, at):
    which = lax.broadcasted_iota(jnp.int32, parts.shape, 0)
    return jnp.sum(jnp.where(which == at, own[None], parts.astype(F32)), axis=0)


def silu_slope(values):
    sigma = jax.nn.sigmoid(values)
    return sigma * (1.0 + values * (1.0 - sigma))


def per_device(encodings, hidden_pre, cotangent, out_weights, out_contacts, in_contacts):
    position = lax.axis_index("blk")
    place = jnp.stack(
        [position // (NZ * NC), position // NC % NZ, position % NC, lax.axis_index("smp")]
    ).astype(jnp.int32)
    out_index, in_index = out_contacts.T, in_contacts.T
    pre = hidden_pre.astype(F32)

    activation = jax.nn.silu(pre).astype(BF16).T
    arrived = [moved(activation, dx=d) for d in range(1, NX)]
    along_x = jnp.stack([activation] + arrived)
    act_own = lax.all_gather(along_x, "blk", axis_index_groups=LINES)
    act_own = act_own.reshape(NZ * NX, BS, -1)
    send, keep = hidden_sums(place, out_index, cotangent, out_weights, arrived[0])

    by_x = core_sums(place, keep, moved(send, dc=1))
    by_z, own_z = line_sums(place, by_x[0], *[moved(by_x[d], dx=d) for d in range(1, NX)])
    got = lax.all_to_all(by_z, "blk", 0, 0, axis_index_groups=LINES)

    act_own = after(act_own, own_z)
    terms, done = out_terms(place, out_index, cotangent, act_own, moved(act_own, dc=1))
    grad_act = sum_parts(got, after(own_z, done), place[1])
    slope = silu_slope(pre)
    first = (grad_act[:FIRST] * slope[:FIRST]).astype(BF16)
    last = (grad_act[FIRST:] * slope[FIRST:]).astype(BF16)
    out_grad = lax.psum_scatter(after(terms, last), "smp", scatter_dimension=0, tiled=True)

    last_x = jnp.stack([last] + [moved(last, dx=d) for d in range(1, NX)])
    copies = jnp.broadcast_to(first, (NZ, *first.shape))
    along_z = lax.all_to_all(copies, "blk", 0, 0, axis_index_groups=LINES)
    own = [along_z] + [moved(along_z, dx=d) for d in range(1, NX)]
    copies = jnp.broadcast_to(last_x, (NZ, *last_x.shape))
    last_own = lax.all_to_all(copies, "blk", 0, 0, axis_index_groups=LINES)
    parts = own + [moved(part, dc=1) for part in own] + [last_own, moved(last_own, dc=1)]

    mine, *away = in_terms(place, in_index, encodings, parts)
    in_grad = sum((moved_smp(a, d + 1).astype(F32) for d, a in enumerate(away)), mine).astype(BF16)
    return (out_grad, in_grad)


def solution(mesh):
    in_specs = (
        P("smp", "blk"),
        P("smp", "blk"),
        P("smp", "blk"),
        P("blk", None, None),
        P("blk", None),
        P("blk", None),
    )
    out_specs = (P(("blk", "smp"), None, None), P(("blk", "smp"), None, None))
    return jax.shard_map(
        per_device, mesh=mesh, in_specs=in_specs, out_specs=out_specs, check_vma=False
    )
```

```python
import jax
import jax.numpy as jnp
from jax import lax
from jax.experimental import pallas as pl
from jax.experimental.pallas import tpu as pltpu
from jax.sharding import PartitionSpec as P

BF16 = jnp.bfloat16
F32 = jnp.float32
NX, NZ, NC, NY = 4, 8, 2, 4
BS = 128
STEP_BLOCKS = 28
OUT_STEP = 28
FIRST, LAST = 176, 80
CORE_STEP = 2


def index_of(x, z, core):
    return ((x % NX) * NZ + z % NZ) * NC + core % NC


def moved(value, dx=0, dz=0, dc=0):
    pairs = [
        (index_of(x, z, c), index_of(x + dx, z + dz, c + dc))
        for x in range(NX)
        for z in range(NZ)
        for c in range(NC)
    ]
    return lax.ppermute(value, "blk", pairs)


def moved_smp(value, dy):
    return lax.ppermute(value, "smp", [(i, (i + dy) % NY) for i in range(NY)])


LINES = [[index_of(x, z, c) for z in range(NZ)] for x in range(NX) for c in range(NC)]


def params(mib):
    return pltpu.CompilerParams(vmem_limit_bytes=mib * 2**20)


def contract(lhs, rhs, over):
    return lax.dot_general(lhs, rhs, ((over[:1], over[1:]), ((), ())), preferred_element_type=F32)


def after(value, other, mib=56):
    anywhere = pl.BlockSpec(memory_space=pl.ANY)
    return pl.pallas_call(
        lambda *refs: None,
        in_specs=[anywhere, anywhere],
        out_specs=anywhere,
        out_shape=jax.ShapeDtypeStruct(value.shape, value.dtype),
        input_output_aliases={0: 0},
        name="after",
    )(value, other)


def hidden_kernel(place, contacts, cot_ref, weight_ref, before_ref, send_ref, keep_ref, total):
    del before_ref
    step = pl.program_id(0)
    core = place[2]

    @pl.when(step == 0)
    def _():
        total[...] = jnp.zeros_like(total)

    for o in range(STEP_BLOCKS):
        cot = cot_ref[:, o * BS : (o + 1) * BS]
        weights = weight_ref[2 * o : 2 * o + 2].reshape(2 * BS, BS)
        terms = contract(cot, weights, (1, 1))
        for m in range(2):
            k = contacts[m, step * STEP_BLOCKS + o]
            total[k] += terms[:, m * BS : (m + 1) * BS]

    @pl.when(step == pl.num_programs(0) - 1)
    def _():
        def write(p, carry):
            send_ref[p] = total[2 * p + 1 - core].astype(BF16)
            keep_ref[p] = total[2 * p + core]
            return carry

        lax.fori_loop(0, NX * NZ, write, 0)


def hidden_sums(place, contacts, cotangent, weights, before):
    rows = cotangent.shape[0]
    count = NX * NZ
    steps = weights.shape[0] // (2 * STEP_BLOCKS)
    return pl.pallas_call(
        hidden_kernel,
        grid_spec=pltpu.PrefetchScalarGridSpec(
            num_scalar_prefetch=2,
            grid=(steps,),
            in_specs=[
                pl.BlockSpec((rows, STEP_BLOCKS * BS), lambda g, *_: (0, g)),
                pl.BlockSpec((2 * STEP_BLOCKS, BS, BS), lambda g, *_: (g, 0, 0)),
                pl.BlockSpec(memory_space=pl.ANY),
            ],
            out_specs=[
                pl.BlockSpec((count, rows, BS), lambda g, *_: (0, 0, 0)),
                pl.BlockSpec((count, rows, BS), lambda g, *_: (0, 0, 0)),
            ],
            scratch_shapes=[pltpu.VMEM((2 * count, rows, BS), F32)],
        ),
        out_shape=[
            jax.ShapeDtypeStruct((count, rows, BS), BF16),
            jax.ShapeDtypeStruct((count, rows, BS), F32),
        ],
        compiler_params=params(44),
        cost_estimate=pl.CostEstimate(flops=3 * 10**9, bytes_accessed=2**24, transcendentals=0),
        name="hidden_sums",
    )(place, contacts, cotangent, weights, before)


def core_kernel(place, keep_ref, got_ref, *outs):
    x = place[0]
    for d in range(NX):
        at = (x + d) & (NX - 1)
        for n in range(CORE_STEP):
            outs[d][n] = (keep_ref[at, n] + got_ref[at, n].astype(F32)).astype(outs[d].dtype)


def core_sums(place, keep, got):
    rows = keep.shape[1]
    spec = pl.BlockSpec((NX, CORE_STEP, rows, BS), lambda g, *_: (0, g, 0, 0))
    return pl.pallas_call(
        core_kernel,
        grid_spec=pltpu.PrefetchScalarGridSpec(
            num_scalar_prefetch=1,
            grid=(NZ // CORE_STEP,),
            in_specs=[spec, spec],
            out_specs=[pl.BlockSpec((CORE_STEP, rows, BS), lambda g, *_: (g, 0, 0))] * NX,
        ),
        out_shape=[
            jax.ShapeDtypeStruct((NZ, rows, BS), BF16 if d else F32) for d in range(NX)
        ],
        compiler_params=params(16),
        cost_estimate=pl.CostEstimate(flops=10**6, bytes_accessed=2**23, transcendentals=0),
        name="core_sums",
    )(place, keep.reshape(NX, NZ, rows, BS), got.reshape(NX, NZ, rows, BS))


def line_kernel(place, keep_ref, a_ref, b_ref, c_ref, send_ref, own_ref):
    def total(at):
        return keep_ref[at] + a_ref[at].astype(F32) + b_ref[at].astype(F32) + c_ref[at].astype(F32)

    for at in range(NZ):
        send_ref[at] = total(at).astype(BF16)
    own_ref[...] = total(place[1])


def line_sums(place, keep, *got):
    rows = keep.shape[1]
    whole = pl.BlockSpec(memory_space=pltpu.VMEM)
    return pl.pallas_call(
        line_kernel,
        in_specs=[pl.BlockSpec(memory_space=pltpu.SMEM)] + [whole] * NX,
        out_specs=[whole] * 2,
        out_shape=[
            jax.ShapeDtypeStruct((NZ, rows, BS), BF16),
            jax.ShapeDtypeStruct((rows, BS), F32),
        ],
        compiler_params=params(8),
        cost_estimate=pl.CostEstimate(flops=10**6, bytes_accessed=2**22, transcendentals=0),
        name="line_sums",
    )(place, keep, *got)


def out_kernel(place, contacts, cot_ref, own_ref, other_ref, out_ref, mark_ref, held, sems):
    step = pl.program_id(0)
    x, core = place[0], place[2]

    @pl.when(step == 0)
    def _():
        copies = [
            pltpu.make_async_copy(own_ref, held.at[core], sems.at[0]),
            pltpu.make_async_copy(other_ref, held.at[1 - core], sems.at[1]),
        ]
        for copy in copies:
            copy.start()
        for copy in copies:
            copy.wait()
        mark_ref[...] = jnp.zeros_like(mark_ref)

    def block(k):
        return held[k & 1, ((k >> 1) & (NZ - 1)) * NX + ((x - (k >> 4)) & (NX - 1))]

    for o in range(OUT_STEP):
        pair = [block(contacts[m, step * OUT_STEP + o]) for m in range(2)]
        cot = cot_ref[:, o * BS : (o + 1) * BS]
        terms = contract(jnp.concatenate(pair), cot, (1, 0)).astype(BF16)
        out_ref[2 * o : 2 * o + 2] = terms.reshape(2, BS, BS)


def out_terms(place, contacts, cotangent, own, other):
    rows = cotangent.shape[0]
    count = contacts.shape[1]
    return pl.pallas_call(
        out_kernel,
        grid_spec=pltpu.PrefetchScalarGridSpec(
            num_scalar_prefetch=2,
            grid=(count // OUT_STEP,),
            in_specs=[
                pl.BlockSpec((rows, OUT_STEP * BS), lambda g, *_: (0, g)),
                pl.BlockSpec(memory_space=pl.ANY),
                pl.BlockSpec(memory_space=pl.ANY),
            ],
            out_specs=[
                pl.BlockSpec((2 * OUT_STEP, BS, BS), lambda g, *_: (g, 0, 0)),
                pl.BlockSpec((8, BS), lambda g, *_: (0, 0)),
            ],
            scratch_shapes=[
                pltpu.VMEM((NC, NX * NZ, BS, rows), BF16),
                pltpu.SemaphoreType.DMA((2,)),
            ],
        ),
        out_shape=[
            jax.ShapeDtypeStruct((2 * count, BS, BS), BF16),
            jax.ShapeDtypeStruct((8, BS), F32),
        ],
        compiler_params=params(48),
        cost_estimate=pl.CostEstimate(flops=3 * 10**9, bytes_accessed=2**24, transcendentals=0),
        name="out_terms",
    )(place, contacts, cotangent, own, other)


def in_kernel(place, contacts, enc_ref, *refs):
    firsts, lasts = refs[: NC * NX], refs[NC * NX : NC * NX + NC]
    outs, (held, made, sems) = refs[NC * NX + NC :][:NY], refs[NC * NX + NC + NY :]
    x, core, y = place[0], place[2], place[3]
    copies = []
    for n, first in enumerate(firsts):
        last = lasts[n // NX].at[:, n % NX]
        copies += [
            pltpu.make_async_copy(first, held.at[n, :, pl.ds(0, FIRST)], sems.at[n, 0]),
            pltpu.make_async_copy(last, held.at[n, :, pl.ds(FIRST, LAST)], sems.at[n, 1]),
        ]
    for copy in copies:
        copy.start()
    for copy in copies:
        copy.wait()
    per_in, count = contacts.shape
    for i in range(count):
        turned = enc_ref[:, i * BS : (i + 1) * BS].T
        for m in range(per_in):
            k = contacts[m, i]
            slot = ((k & 1) ^ core) * NX + ((x - (k >> 4)) & (NX - 1))
            made[i * per_in + m] = contract(turned, held[slot, (k >> 1) & (NZ - 1)], (1, 0))
    each = count * per_in // NY
    for d in range(NY):
        first = ((y + d) & (NY - 1)) * each
        for n in range(each):
            outs[d][n] = made[first + n].astype(outs[d].dtype)


def in_terms(place, contacts, encodings, parts):
    rows = encodings.shape[0]
    per_in, count = contacts.shape
    each = per_in * count // NY
    smem = pl.BlockSpec(memory_space=pltpu.SMEM)
    whole = pl.BlockSpec(memory_space=pltpu.VMEM)
    return pl.pallas_call(
        in_kernel,
        in_specs=[smem, smem, whole] + [pl.BlockSpec(memory_space=pl.ANY)] * (NC * NX + NC),
        out_specs=[whole] * NY,
        scratch_shapes=[
            pltpu.VMEM((NC * NX, NZ, rows, BS), BF16),
            pltpu.VMEM((per_in * count, BS, BS), F32),
            pltpu.SemaphoreType.DMA((NC * NX, 2)),
        ],
        out_shape=[jax.ShapeDtypeStruct((each, BS, BS), BF16 if d else F32) for d in range(NY)],
        compiler_params=params(14),
        cost_estimate=pl.CostEstimate(flops=5 * 10**8, bytes_accessed=2**23, transcendentals=0),
        name="in_terms",
    )(place, contacts, encodings, *parts)


def sum_parts(parts, own, at):
    which = lax.broadcasted_iota(jnp.int32, parts.shape, 0)
    return jnp.sum(jnp.where(which == at, own[None], parts.astype(F32)), axis=0)


def silu_slope(values):
    sigma = jax.nn.sigmoid(values)
    return sigma * (1.0 + values * (1.0 - sigma))


def per_device(encodings, hidden_pre, cotangent, out_weights, out_contacts, in_contacts):
    position = lax.axis_index("blk")
    place = jnp.stack(
        [position // (NZ * NC), position // NC % NZ, position % NC, lax.axis_index("smp")]
    ).astype(jnp.int32)
    out_index, in_index = out_contacts.T, in_contacts.T
    pre = hidden_pre.astype(F32)

    activation = jax.nn.silu(pre).astype(BF16).T
    arrived = [moved(activation, dx=d) for d in range(1, NX)]
    along_x = jnp.stack([activation] + arrived)
    act_own = lax.all_gather(along_x, "blk", axis_index_groups=LINES)
    act_own = act_own.reshape(NZ * NX, BS, -1)
    send, keep = hidden_sums(place, out_index, cotangent, out_weights, arrived[0])

    by_x = core_sums(place, keep, moved(send, dc=1))
    by_z, own_z = line_sums(place, by_x[0], *[moved(by_x[d], dx=d) for d in range(1, NX)])
    got = lax.all_to_all(by_z, "blk", 0, 0, axis_index_groups=LINES)

    act_own = after(act_own, own_z)
    terms, done = out_terms(place, out_index, cotangent, act_own, moved(act_own, dc=1))
    grad_act = sum_parts(got, after(own_z, done), place[1])
    slope = silu_slope(pre)
    first = (grad_act[:FIRST] * slope[:FIRST]).astype(BF16)
    last = (grad_act[FIRST:] * slope[FIRST:]).astype(BF16)
    out_grad = lax.psum_scatter(after(terms, last), "smp", scatter_dimension=0, tiled=True)

    last_x = jnp.stack([last] + [moved(last, dx=d) for d in range(1, NX)])
    copies = jnp.broadcast_to(first, (NZ, *first.shape))
    along_z = lax.all_to_all(copies, "blk", 0, 0, axis_index_groups=LINES)
    own = [along_z] + [moved(along_z, dx=d) for d in range(1, NX)]
    copies = jnp.broadcast_to(last_x, (NZ, *last_x.shape))
    last_own = lax.all_to_all(copies, "blk", 0, 0, axis_index_groups=LINES)
    parts = own + [moved(part, dc=1) for part in own] + [last_own, moved(last_own, dc=1)]

    mine, *away = in_terms(place, in_index, encodings, parts)
    came = [moved_smp(away[d - 1], d) for d in (2, 1, 3)]
    in_grad = sum((part.astype(F32) for part in came), mine).astype(BF16)
    return (out_grad, in_grad)


def solution(mesh):
    in_specs = (
        P("smp", "blk"),
        P("smp", "blk"),
        P("smp", "blk"),
        P("blk", None, None),
        P("blk", None),
        P("blk", None),
    )
    out_specs = (P(("blk", "smp"), None, None), P(("blk", "smp"), None, None))
    return jax.shard_map(
        per_device, mesh=mesh, in_specs=in_specs, out_specs=out_specs, check_vma=False
    )
```

```python
import jax
import jax.numpy as jnp
from jax import lax
from jax.experimental import pallas as pl
from jax.experimental.pallas import tpu as pltpu
from jax.sharding import PartitionSpec as P

BF16 = jnp.bfloat16
F32 = jnp.float32
NX, NZ, NC, NY = 4, 8, 2, 4
BS = 128
STEP_BLOCKS = 28
OUT_STEP = 28
FIRST, LAST = 160, 96
CORE_STEP = 2


def index_of(x, z, core):
    return ((x % NX) * NZ + z % NZ) * NC + core % NC


def moved(value, dx=0, dz=0, dc=0):
    pairs = [
        (index_of(x, z, c), index_of(x + dx, z + dz, c + dc))
        for x in range(NX)
        for z in range(NZ)
        for c in range(NC)
    ]
    return lax.ppermute(value, "blk", pairs)


def moved_smp(value, dy):
    return lax.ppermute(value, "smp", [(i, (i + dy) % NY) for i in range(NY)])


LINES = [[index_of(x, z, c) for z in range(NZ)] for x in range(NX) for c in range(NC)]


def params(mib):
    return pltpu.CompilerParams(vmem_limit_bytes=mib * 2**20)


def contract(lhs, rhs, over):
    return lax.dot_general(lhs, rhs, ((over[:1], over[1:]), ((), ())), preferred_element_type=F32)


def after(value, other, mib=56):
    anywhere = pl.BlockSpec(memory_space=pl.ANY)
    return pl.pallas_call(
        lambda *refs: None,
        in_specs=[anywhere, anywhere],
        out_specs=anywhere,
        out_shape=jax.ShapeDtypeStruct(value.shape, value.dtype),
        input_output_aliases={0: 0},
        name="after",
    )(value, other)


def hidden_kernel(place, contacts, cot_ref, weight_ref, before_ref, send_ref, keep_ref, total):
    del before_ref
    step = pl.program_id(0)
    core = place[2]

    @pl.when(step == 0)
    def _():
        total[...] = jnp.zeros_like(total)

    for o in range(STEP_BLOCKS):
        cot = cot_ref[:, o * BS : (o + 1) * BS]
        weights = weight_ref[2 * o : 2 * o + 2].reshape(2 * BS, BS)
        terms = contract(cot, weights, (1, 1))
        for m in range(2):
            k = contacts[m, step * STEP_BLOCKS + o]
            total[k] += terms[:, m * BS : (m + 1) * BS]

    @pl.when(step == pl.num_programs(0) - 1)
    def _():
        def write(p, carry):
            send_ref[p] = total[2 * p + 1 - core].astype(BF16)
            keep_ref[p] = total[2 * p + core]
            return carry

        lax.fori_loop(0, NX * NZ, write, 0)


def hidden_sums(place, contacts, cotangent, weights, before):
    rows = cotangent.shape[0]
    count = NX * NZ
    steps = weights.shape[0] // (2 * STEP_BLOCKS)
    return pl.pallas_call(
        hidden_kernel,
        grid_spec=pltpu.PrefetchScalarGridSpec(
            num_scalar_prefetch=2,
            grid=(steps,),
            in_specs=[
                pl.BlockSpec((rows, STEP_BLOCKS * BS), lambda g, *_: (0, g)),
                pl.BlockSpec((2 * STEP_BLOCKS, BS, BS), lambda g, *_: (g, 0, 0)),
                pl.BlockSpec(memory_space=pl.ANY),
            ],
            out_specs=[
                pl.BlockSpec((count, rows, BS), lambda g, *_: (0, 0, 0)),
                pl.BlockSpec((count, rows, BS), lambda g, *_: (0, 0, 0)),
            ],
            scratch_shapes=[pltpu.VMEM((2 * count, rows, BS), F32)],
        ),
        out_shape=[
            jax.ShapeDtypeStruct((count, rows, BS), BF16),
            jax.ShapeDtypeStruct((count, rows, BS), F32),
        ],
        compiler_params=params(44),
        cost_estimate=pl.CostEstimate(flops=3 * 10**9, bytes_accessed=2**24, transcendentals=0),
        name="hidden_sums",
    )(place, contacts, cotangent, weights, before)


def core_kernel(place, keep_ref, got_ref, *outs):
    x = place[0]
    for d in range(NX):
        at = (x + d) & (NX - 1)
        for n in range(CORE_STEP):
            outs[d][n] = (keep_ref[at, n] + got_ref[at, n].astype(F32)).astype(outs[d].dtype)


def core_sums(place, keep, got):
    rows = keep.shape[1]
    spec = pl.BlockSpec((NX, CORE_STEP, rows, BS), lambda g, *_: (0, g, 0, 0))
    return pl.pallas_call(
        core_kernel,
        grid_spec=pltpu.PrefetchScalarGridSpec(
            num_scalar_prefetch=1,
            grid=(NZ // CORE_STEP,),
            in_specs=[spec, spec],
            out_specs=[pl.BlockSpec((CORE_STEP, rows, BS), lambda g, *_: (g, 0, 0))] * NX,
        ),
        out_shape=[
            jax.ShapeDtypeStruct((NZ, rows, BS), BF16 if d else F32) for d in range(NX)
        ],
        compiler_params=params(16),
        cost_estimate=pl.CostEstimate(flops=10**6, bytes_accessed=2**23, transcendentals=0),
        name="core_sums",
    )(place, keep.reshape(NX, NZ, rows, BS), got.reshape(NX, NZ, rows, BS))


def line_kernel(place, keep_ref, a_ref, b_ref, c_ref, send_ref, own_ref):
    def total(at):
        return keep_ref[at] + a_ref[at].astype(F32) + b_ref[at].astype(F32) + c_ref[at].astype(F32)

    for at in range(NZ):
        send_ref[at] = total(at).astype(BF16)
    own_ref[...] = total(place[1])


def line_sums(place, keep, *got):
    rows = keep.shape[1]
    whole = pl.BlockSpec(memory_space=pltpu.VMEM)
    return pl.pallas_call(
        line_kernel,
        in_specs=[pl.BlockSpec(memory_space=pltpu.SMEM)] + [whole] * NX,
        out_specs=[whole] * 2,
        out_shape=[
            jax.ShapeDtypeStruct((NZ, rows, BS), BF16),
            jax.ShapeDtypeStruct((rows, BS), F32),
        ],
        compiler_params=params(8),
        cost_estimate=pl.CostEstimate(flops=10**6, bytes_accessed=2**22, transcendentals=0),
        name="line_sums",
    )(place, keep, *got)


def out_kernel(place, contacts, cot_ref, own_ref, other_ref, out_ref, mark_ref, held, sems):
    step = pl.program_id(0)
    x, core = place[0], place[2]

    @pl.when(step == 0)
    def _():
        copies = [
            pltpu.make_async_copy(own_ref, held.at[core], sems.at[0]),
            pltpu.make_async_copy(other_ref, held.at[1 - core], sems.at[1]),
        ]
        for copy in copies:
            copy.start()
        for copy in copies:
            copy.wait()
        mark_ref[...] = jnp.zeros_like(mark_ref)

    def block(k):
        return held[k & 1, ((k >> 1) & (NZ - 1)) * NX + ((x - (k >> 4)) & (NX - 1))]

    for o in range(OUT_STEP):
        pair = [block(contacts[m, step * OUT_STEP + o]) for m in range(2)]
        cot = cot_ref[:, o * BS : (o + 1) * BS]
        terms = contract(jnp.concatenate(pair), cot, (1, 0)).astype(BF16)
        out_ref[2 * o : 2 * o + 2] = terms.reshape(2, BS, BS)


def out_terms(place, contacts, cotangent, own, other):
    rows = cotangent.shape[0]
    count = contacts.shape[1]
    return pl.pallas_call(
        out_kernel,
        grid_spec=pltpu.PrefetchScalarGridSpec(
            num_scalar_prefetch=2,
            grid=(count // OUT_STEP,),
            in_specs=[
                pl.BlockSpec((rows, OUT_STEP * BS), lambda g, *_: (0, g)),
                pl.BlockSpec(memory_space=pl.ANY),
                pl.BlockSpec(memory_space=pl.ANY),
            ],
            out_specs=[
                pl.BlockSpec((2 * OUT_STEP, BS, BS), lambda g, *_: (g, 0, 0)),
                pl.BlockSpec((8, BS), lambda g, *_: (0, 0)),
            ],
            scratch_shapes=[
                pltpu.VMEM((NC, NX * NZ, BS, rows), BF16),
                pltpu.SemaphoreType.DMA((2,)),
            ],
        ),
        out_shape=[
            jax.ShapeDtypeStruct((2 * count, BS, BS), BF16),
            jax.ShapeDtypeStruct((8, BS), F32),
        ],
        compiler_params=params(48),
        cost_estimate=pl.CostEstimate(flops=3 * 10**9, bytes_accessed=2**24, transcendentals=0),
        name="out_terms",
    )(place, contacts, cotangent, own, other)


def in_kernel(place, contacts, enc_ref, *refs):
    firsts, lasts = refs[: NC * NX], refs[NC * NX : NC * NX + NC]
    outs, (held, made, sems) = refs[NC * NX + NC :][:NY], refs[NC * NX + NC + NY :]
    x, core, y = place[0], place[2], place[3]
    copies = []
    for n, first in enumerate(firsts):
        last = lasts[n // NX].at[:, n % NX]
        copies += [
            pltpu.make_async_copy(first, held.at[n, :, pl.ds(0, FIRST)], sems.at[n, 0]),
            pltpu.make_async_copy(last, held.at[n, :, pl.ds(FIRST, LAST)], sems.at[n, 1]),
        ]
    for copy in copies:
        copy.start()
    for copy in copies:
        copy.wait()
    per_in, count = contacts.shape
    for i in range(count):
        turned = enc_ref[:, i * BS : (i + 1) * BS].T
        for m in range(per_in):
            k = contacts[m, i]
            slot = ((k & 1) ^ core) * NX + ((x - (k >> 4)) & (NX - 1))
            made[i * per_in + m] = contract(turned, held[slot, (k >> 1) & (NZ - 1)], (1, 0))
    each = count * per_in // NY
    for d in range(NY):
        first = ((y + d) & (NY - 1)) * each
        for n in range(each):
            outs[d][n] = made[first + n].astype(outs[d].dtype)


def in_terms(place, contacts, encodings, parts):
    rows = encodings.shape[0]
    per_in, count = contacts.shape
    each = per_in * count // NY
    smem = pl.BlockSpec(memory_space=pltpu.SMEM)
    whole = pl.BlockSpec(memory_space=pltpu.VMEM)
    return pl.pallas_call(
        in_kernel,
        in_specs=[smem, smem, whole] + [pl.BlockSpec(memory_space=pl.ANY)] * (NC * NX + NC),
        out_specs=[whole] * NY,
        scratch_shapes=[
            pltpu.VMEM((NC * NX, NZ, rows, BS), BF16),
            pltpu.VMEM((per_in * count, BS, BS), F32),
            pltpu.SemaphoreType.DMA((NC * NX, 2)),
        ],
        out_shape=[jax.ShapeDtypeStruct((each, BS, BS), BF16 if d else F32) for d in range(NY)],
        compiler_params=params(14),
        cost_estimate=pl.CostEstimate(flops=5 * 10**8, bytes_accessed=2**23, transcendentals=0),
        name="in_terms",
    )(place, contacts, encodings, *parts)


def sum_parts(parts, own, at):
    which = lax.broadcasted_iota(jnp.int32, parts.shape, 0)
    return jnp.sum(jnp.where(which == at, own[None], parts.astype(F32)), axis=0)


def silu_slope(values):
    sigma = jax.nn.sigmoid(values)
    return sigma * (1.0 + values * (1.0 - sigma))


def per_device(encodings, hidden_pre, cotangent, out_weights, out_contacts, in_contacts):
    position = lax.axis_index("blk")
    place = jnp.stack(
        [position // (NZ * NC), position // NC % NZ, position % NC, lax.axis_index("smp")]
    ).astype(jnp.int32)
    out_index, in_index = out_contacts.T, in_contacts.T
    pre = hidden_pre.astype(F32)

    activation = jax.nn.silu(pre).astype(BF16).T
    arrived = [moved(activation, dx=d) for d in range(1, NX)]
    along_x = jnp.stack([activation] + arrived)
    act_own = lax.all_gather(along_x, "blk", axis_index_groups=LINES)
    act_own = act_own.reshape(NZ * NX, BS, -1)
    send, keep = hidden_sums(place, out_index, cotangent, out_weights, arrived[0])

    by_x = core_sums(place, keep, moved(send, dc=1))
    by_z, own_z = line_sums(place, by_x[0], *[moved(by_x[d], dx=d) for d in range(1, NX)])
    got = lax.all_to_all(by_z, "blk", 0, 0, axis_index_groups=LINES)

    act_own = after(act_own, own_z)
    terms, done = out_terms(place, out_index, cotangent, act_own, moved(act_own, dc=1))
    grad_act = sum_parts(got, after(own_z, done), place[1])
    slope = silu_slope(pre)
    first = (grad_act[:FIRST] * slope[:FIRST]).astype(BF16)
    last = (grad_act[FIRST:] * slope[FIRST:]).astype(BF16)
    out_grad = lax.psum_scatter(after(terms, last), "smp", scatter_dimension=0, tiled=True)

    last_x = jnp.stack([last] + [moved(last, dx=d) for d in range(1, NX)])
    copies = jnp.broadcast_to(first, (NZ, *first.shape))
    along_z = lax.all_to_all(copies, "blk", 0, 0, axis_index_groups=LINES)
    own = [along_z] + [moved(along_z, dx=d) for d in range(1, NX)]
    copies = jnp.broadcast_to(last_x, (NZ, *last_x.shape))
    last_own = lax.all_to_all(copies, "blk", 0, 0, axis_index_groups=LINES)
    parts = own + [moved(part, dc=1) for part in own] + [last_own, moved(last_own, dc=1)]

    mine, *away = in_terms(place, in_index, encodings, parts)
    came = [moved_smp(away[d - 1], d) for d in (2, 1, 3)]
    in_grad = sum((part.astype(F32) for part in came), mine).astype(BF16)
    return (out_grad, in_grad)


def solution(mesh):
    in_specs = (
        P("smp", "blk"),
        P("smp", "blk"),
        P("smp", "blk"),
        P("blk", None, None),
        P("blk", None),
        P("blk", None),
    )
    out_specs = (P(("blk", "smp"), None, None), P(("blk", "smp"), None, None))
    return jax.shard_map(
        per_device, mesh=mesh, in_specs=in_specs, out_specs=out_specs, check_vma=False
    )
```
